256 devices in a mesh: term: 16 (over y, x_lo, core), topic: 16 (over x_hi, z).
Axes of the slice: x: 4 (x_hi: 2, x_lo: 2; x = x_hi * 2 + x_lo), y: 4, z: 8, core: 2. Of those that a mesh axis runs over, the one named last changes fastest.
Arguments:
- factor: bfloat16 [131072, 2048], P('term', 'topic'), may hold values from 1e-06 to 0.05, as said below
- tile_values: bfloat16 [131072, 128], P('term'), may hold values from 0.049804688 to 1
- tile_docs: int32 [16, 128], P('term'), may hold values from 0 to 255, as said below
- codes: float32 [2048, 256], P('topic', 'term'), may hold values from 0.1 to 2
- gram_stat: float32 [2048, 2048], P('topic', 'term'), may hold values from 0 to 4
- data_stat: float32 [131072, 2048], P('term', 'topic'), may hold values from 0 to 0.4
Outputs:
- codes_out: float32 [2048, 256], P('topic', 'term')
- gram_new: float32 [2048, 2048], P('topic', 'term')
- data_new: float32 [131072, 2048], P('term', 'topic')
The draws below stay inside these ranges and needn't reach their ends.
Inputs may be any that keep to these rules, and one draw needn't show every extreme that they name: `tile_docs`: each row lists 128 different document numbers. `factor`: positive entries.
All inputs are finite; a program needn't handle non-finite values.
Results may differ from the reference program's by a relative error of at most 0.0003.
Values may be sent and summed in bfloat16 or wider, within the bound.
A program may use at most 128 MiB of HBM per device.

```python
import math
import jax
import jax.numpy as jnp
from jax import lax

SLAB = 8192
TILE = 128
ITERS = 3
TERMS = 131072
TOPICS = 2048
DOCS = 256
SLABS = 16


def draw_tile_docs(key, part):
    slab_keys = jax.random.split(jax.random.fold_in(key, 11), SLABS)
    picked = jax.vmap(lambda slab_key: jax.random.permutation(slab_key, DOCS)[:TILE])(slab_keys)
    return picked.astype(jnp.int32)


def draw_factor(key, part):
    groups = max(TOPICS // 16, 1)
    term_group = jax.random.randint(jax.random.fold_in(key, 21), (TERMS, 1), 0, groups)
    topic_group = jax.random.randint(jax.random.fold_in(key, 22), (1, TOPICS), 0, groups)
    exponent = jnp.clip(jax.random.normal(jax.random.fold_in(key, 23), (TERMS, TOPICS), jnp.float32), -2.5, 2.5)
    magnitude = jnp.where(term_group == topic_group, jnp.float32(0.004), jnp.float32(0.004 / 300.0))
    return (magnitude * jnp.exp(exponent)).astype(jnp.bfloat16)


def levels(own_key, extent, cuts, least, largest):
    def one(dim, shards_of):
        draws = jax.random.uniform(jax.random.fold_in(jax.random.fold_in(own_key, 6), dim), (shards_of,), jnp.float32, least / len(cuts), largest / len(cuts))
        return jnp.repeat(jnp.exp(draws), extent[dim] // shards_of).reshape((-1,) + (1,) * (len(extent) - dim - 1))

    level = one(*cuts[0])
    for cut in cuts[1:]:
        level = level * one(*cut)
    return level


def setup_inputs(seed: int = 0) -> dict:
    arg_keys = jax.random.split(jax.random.key(seed), 7)
    return {
        "factor": draw_factor(jax.random.fold_in(arg_keys[6], 71), 0),
        "tile_values": jnp.clip(jnp.exp(math.log(1.0) - 2.9996462 * jax.random.uniform(arg_keys[1], (TERMS, TILE), jnp.float32) ** levels(arg_keys[1], (TERMS, TILE), ((0, 16),), -0.2, 0.2)), 0.049804688, 1.0).astype(jnp.bfloat16),
        "tile_docs": draw_tile_docs(jax.random.fold_in(arg_keys[6], 71), 0),
        "codes": jnp.clip(jnp.exp(math.log(2.0) - 2.9957323 * jax.random.uniform(arg_keys[3], (TOPICS, DOCS), jnp.float32) ** levels(arg_keys[3], (TOPICS, DOCS), ((0, 16), (1, 16)), -0.2, 0.2)), 0.1, 2.0),
        "gram_stat": jnp.clip(4.0 * jax.random.uniform(arg_keys[4], (TOPICS, TOPICS), jnp.float32) ** levels(arg_keys[4], (TOPICS, TOPICS), ((0, 16), (1, 16)), -0.2, 0.2), 0.0, 4.0),
        "data_stat": jnp.clip(0.4 * jax.random.uniform(arg_keys[5], (TERMS, TOPICS), jnp.float32) ** levels(arg_keys[5], (TERMS, TOPICS), ((0, 16), (1, 16)), -0.2, 0.2), 0.0, 0.4),
    }


EPSILON = 1e-6
DECAY = 0.5


def reference(factor, tile_values, tile_docs, codes, gram_stat, data_stat):
    onehot = (tile_docs[:, :, None] == jnp.arange(DOCS, dtype=jnp.int32)[None, None, :]).astype(jnp.float32)
    tiles = tile_values.reshape(SLABS, SLAB, TILE).astype(jnp.float32)
    batch = jnp.einsum("svt,stb->svb", tiles, onehot).astype(jnp.bfloat16).reshape(SLABS * SLAB, DOCS)
    gram = jnp.dot(factor.T, factor, preferred_element_type=jnp.float32)
    data = jnp.dot(factor.T, batch, preferred_element_type=jnp.float32)
    current = codes
    for update in range(ITERS):
        applied = jnp.dot(gram, current, precision=lax.Precision.HIGHEST, preferred_element_type=jnp.float32)
        current = current * data / (applied + EPSILON)
    outer = jnp.dot(current, current.T, precision=lax.Precision.HIGHEST, preferred_element_type=jnp.float32)
    gram_new = DECAY * gram_stat + outer / DOCS
    widened = batch.astype(jnp.float32)
    data_new = DECAY * data_stat + jnp.dot(widened, current.T, precision=lax.Precision.HIGHEST, preferred_element_type=jnp.float32) / DOCS
    return current, gram_new, data_new
```

```python
import functools

import jax
import jax.numpy as jnp
from jax import lax
from jax.experimental import pallas as pl
from jax.experimental.pallas import tpu as pltpu
from jax.sharding import PartitionSpec as P

ITERS = 3
EPSILON = 1e-06
DECAY = 0.5
MESH = pl.DeviceIdType.MESH
BF = jnp.bfloat16
F32 = jnp.float32


def split2(value):
    high = value.astype(BF)
    return high, (value - high.astype(F32)).astype(BF)


def dot(left, right):
    return jnp.dot(left, right, preferred_element_type=F32)


def codes_kernel(
    n, factor, tiles, docs, codes, gram_stat,
    codes_out, row_out, gram_out,
    factor_v, tiles_v, xx, xt, own, outgoing, incoming, across, zin,
    gcol, gsend, cbuf, csend, dsend, drecv, fsend, arow, brow,
    local_sem, a2a_send, a2a_recv, core_send, core_recv, y_send, y_recv,
    x_send, x_recv, z_send, z_recv, g_send, g_recv, c_send, c_recv,
    d_send, d_recv, fa_send, fa_recv, fb_send, fb_recv,
):
    rows, topics = factor.shape
    piece = rows // n
    block = codes.shape[0]
    half = n // 2
    ny = n // 4
    d = lax.axis_index("term")
    t = lax.axis_index("topic")
    core = d % 2
    xlo = (d // 2) % 2
    y = d // 4
    sibling = d + 1 - 2 * core
    across_d = d + 2 - 4 * xlo

    barrier = pltpu.get_barrier_semaphore()

    def greet(s, carry):
        pl.semaphore_signal(barrier, 1, device_id={"topic": (t + s) % n}, device_id_type=MESH)
        pl.semaphore_signal(barrier, 1, device_id={"term": (d + s) % n}, device_id_type=MESH)
        return carry

    lax.fori_loop(1, n, greet, 0)

    def greet_senders(s, carry):
        @pl.when((s != d) | (t != d))
        def _():
            pl.semaphore_signal(barrier, 1, device_id={"term": s, "topic": d}, device_id_type=MESH)
        return carry

    lax.fori_loop(0, n, greet_senders, 0)
    load_factor = pltpu.make_async_copy(factor, factor_v, local_sem.at[0])
    load_tiles = pltpu.make_async_copy(tiles, tiles_v, local_sem.at[1])
    load_own = pltpu.make_async_copy(
        factor.at[pl.ds(t * piece, piece)], xx.at[t, pl.ds(core * piece, piece)], a2a_recv.at[t]
    )
    load_own.start()
    load_factor.start()
    load_tiles.start()

    @pl.when(t == d)
    def _():
        pl.semaphore_wait(barrier, 3 * n - 3)

    @pl.when(t != d)
    def _():
        pl.semaphore_wait(barrier, 3 * n - 2)

    def send_piece(s, carry):
        p = (t + s) % n
        pltpu.make_async_remote_copy(
            factor.at[pl.ds(p * piece, piece)],
            xx.at[t, pl.ds(core * piece, piece)],
            a2a_send,
            a2a_recv.at[t],
            device_id={"topic": p},
            device_id_type=MESH,
        ).start()
        return carry

    lax.fori_loop(1, n, send_piece, 0)

    load_factor.wait()
    load_tiles.wait()
    share = jnp.zeros((tiles.shape[1], topics), F32)
    for s in range(n):
        part = tiles_v[s * piece:(s + 1) * piece, :]
        share = share + lax.dot_general(
            part, factor_v[s * piece:(s + 1) * piece, :], (((0,), (0,)), ((), ())),
            preferred_element_type=F32,
        )
    onehot = (
        lax.broadcasted_iota(jnp.int32, (n * block, tiles.shape[1]), 0) == docs[...]
    ).astype(F32).astype(BF)
    high, middle = split2(share)
    low = (share - high.astype(F32) - middle.astype(F32)).astype(BF)
    spread = dot(onehot, high) + dot(onehot, middle) + dot(onehot, low)
    dsend[...] = spread.reshape(n, block, topics)

    def send_share(s, carry):
        target = (d + s) % n
        pltpu.make_async_remote_copy(
            dsend.at[target], drecv.at[d], d_send, d_recv,
            device_id={"term": target}, device_id_type=MESH,
        ).start()
        return carry

    lax.fori_loop(1, n, send_share, 0)
    drecv[d] = dsend[d]

    def place(p, q):
        k = (p + q) % n
        e1 = (p + n - k // 2 - core) % n
        swap = (e1 + half - 1 + core) // n
        i = p + swap * (q - p)
        j = q + swap * (p - q)
        e = (i + n - k // 2 - core) % n
        return k // 4, (k // 2) % 2, e, i, j

    def pair_count(m):
        return (m - (m + core) % 2 + 2) // 2

    def forward(p):
        return pltpu.make_async_remote_copy(
            xx.at[p, pl.ds(core * piece, piece)],
            xx.at[p, pl.ds(core * piece, piece)],
            core_send,
            core_recv.at[p],
            device_id={"term": sibling},
            device_id_type=MESH,
        )

    def arrive(m, carry):
        p = (t + n - m) % n
        mine = xx.at[p, pl.ds(core * piece, piece)]
        pltpu.make_async_copy(mine, mine, a2a_recv.at[p]).wait()
        forward(p).start()
        theirs = xx.at[p, pl.ds((1 - core) * piece, piece)]
        pltpu.make_async_copy(theirs, theirs, core_recv.at[p]).wait()
        xt[p] = xx[p].T

        def pair(s, carry):
            q = (t + n - ((m + core) % 2 + 2 * s)) % n
            y2, x2, e, i, j = place(p, q)
            tile = dot(xt[i], xx[j])

            @pl.when(y2 == y)
            def _():
                own[x2, e] = tile

            @pl.when(y2 != y)
            def _():
                outgoing[y2, x2, e] = tile.astype(BF)
                pltpu.make_async_remote_copy(
                    outgoing.at[y2, x2, e], incoming.at[y, x2, e], y_send, y_recv.at[y, x2, e],
                    device_id={"term": y2 * 4 + xlo * 2 + core}, device_id_type=MESH,
                ).start()

            return carry

        lax.fori_loop(0, pair_count(m), pair, 0)
        return carry

    lax.fori_loop(0, n, arrive, 0)

    def walk(x_want, body):
        def outer_loop(m, carry):
            p = (t + n - m) % n

            def inner(s, carry):
                q = (t + n - ((m + core) % 2 + 2 * s)) % n
                y2, x2, e, i, j = place(p, q)

                @pl.when((y2 == y) & (x2 == x_want))
                def _():
                    body(e, i, j)

                return carry

            lax.fori_loop(0, pair_count(m), inner, 0)
            return carry

        lax.fori_loop(0, n, outer_loop, 0)

    def sum_y(x2, e):
        total = own[x2, e]
        for s in range(1, ny):
            y2 = (y + s) % ny
            got = incoming.at[y2, x2, e]
            pltpu.make_async_copy(got, got, y_recv.at[y2, x2, e]).wait()
            total = total + incoming[y2, x2, e].astype(F32)
        return total

    def send_across(e, i, j):
        own[1 - xlo, e] = sum_y(1 - xlo, e)
        pltpu.make_async_remote_copy(
            own.at[1 - xlo, e], across.at[e], x_send, x_recv.at[e],
            device_id={"term": across_d}, device_id_type=MESH,
        ).start()

    def send_tile(e, target):
        @pl.when(target == t)
        def _():
            zin[t] = own[xlo, e]

        @pl.when(target != t)
        def _():
            pltpu.make_async_remote_copy(
                own.at[xlo, e], zin.at[t], z_send, z_recv,
                device_id={"topic": target}, device_id_type=MESH,
            ).start()

    def send_both(e, i, j):
        total = sum_y(xlo, e)
        pltpu.make_async_copy(across.at[e], across.at[e], x_recv.at[e]).wait()
        own[xlo, e] = total + across[e]
        send_tile(e, i)

        @pl.when(i != j)
        def _():
            send_tile(e, j)

    walk(1 - xlo, send_across)
    walk(xlo, send_both)

    zparts = zin.at[pl.ds(0, n - 1)]
    pltpu.make_async_copy(zparts, zparts, z_recv).wait()
    total = zin[0]
    for s in range(1, n):
        total = total + zin[s]
    first_role = (t + n - d // 2 - core) % n

    @pl.when(first_role <= half - core)
    def _():
        high, middle = split2(total.T)
        gsend[:, :topics] = high
        gsend[:, topics:] = middle

    @pl.when(first_role > half - core)
    def _():
        high, middle = split2(total)
        gsend[:, :topics] = high
        gsend[:, topics:] = middle

    position = (d + n - t) % n

    def send_gram(s, carry):
        pltpu.make_async_remote_copy(
            gsend, gcol.at[pl.ds(position * topics, topics)], g_send, g_recv,
            device_id={"term": (d + s) % n}, device_id_type=MESH,
        ).start()
        return carry

    lax.fori_loop(1, n, send_gram, 0)
    gcol[pl.ds(position * topics, topics), :] = gsend[...]

    dparts = drecv.at[pl.ds(0, n - 1)]
    pltpu.make_async_copy(dparts, dparts, d_recv).wait()
    data = drecv[0]
    for s in range(1, n):
        data = data + drecv[s]

    current = codes[...]
    for step in range(ITERS):
        high, middle = split2(current)
        csend[step, :block, :] = high
        csend[step, block:, :] = middle

        def send_codes(s, carry):
            pltpu.make_async_remote_copy(
                csend.at[step],
                cbuf.at[step, :, pl.ds(pl.multiple_of(t * topics, topics), topics)],
                c_send.at[step],
                c_recv.at[step],
                device_id={"topic": (t + s) % n},
                device_id_type=MESH,
            ).start()
            return carry

        lax.fori_loop(1, n, send_codes, 0)
        cbuf[step, :, pl.ds(pl.multiple_of(t * topics, topics), topics)] = csend[step]
        if step == 0:
            gparts = gcol.at[pl.ds(0, (n - 1) * topics)]
            pltpu.make_async_copy(gparts, gparts, g_recv).wait()
        cparts = cbuf.at[step, :, pl.ds(0, (n - 1) * topics)]
        pltpu.make_async_copy(cparts, cparts, c_recv.at[step]).wait()
        product = dot(cbuf[step], gcol[...])
        applied = product[:, :topics] + product[:, topics:]
        applied = applied[:block] + applied[block:]
        current = current * data / (applied + EPSILON)

    codes_out[...] = current
    fsend[...] = current

    def send_row(s, carry):
        pltpu.make_async_remote_copy(
            fsend, arow.at[d], fa_send, fa_recv,
            device_id={"term": (d + s) % n}, device_id_type=MESH,
        ).start()
        return carry

    lax.fori_loop(1, n, send_row, 0)

    def send_column(s, carry):
        target = (t + s) % n

        @pl.when((t != d) | (target != t))
        def _():
            pltpu.make_async_remote_copy(
                fsend, brow.at[d], fb_send, fb_recv,
                device_id={"term": t, "topic": target}, device_id_type=MESH,
            ).start()

        return carry

    lax.fori_loop(0, n, send_column, 0)
    arow[d] = current
    aparts = arow.at[pl.ds(0, n - 1)]
    pltpu.make_async_copy(aparts, aparts, fa_recv).wait()
    whole = arow[...].reshape(n * block, topics)
    row_out[...] = whole

    @pl.when(t == d)
    def _():
        brow[d] = current
        bparts = brow.at[pl.ds(0, n - 1)]
        pltpu.make_async_copy(bparts, bparts, fb_recv).wait()
        pltpu.make_async_copy(bparts, bparts, fb_send).wait()

    @pl.when(t != d)
    def _():
        pltpu.make_async_copy(brow, brow, fb_recv).wait()
        pltpu.make_async_copy(brow, brow, fb_send).wait()

    a_high, a_middle = split2(whole.T)
    b_high, b_middle = split2(brow[...].reshape(n * block, topics))
    outer = dot(a_high, b_high) + (dot(a_high, b_middle) + dot(a_middle, b_high))
    gram_out[...] = DECAY * gram_stat[...] + outer / (n * block)

    sent = factor.at[pl.ds(0, rows - piece)]
    pltpu.make_async_copy(sent, sent, a2a_send).wait()
    pltpu.make_async_copy(factor, factor, core_send).wait()
    for c in range(2):
        @pl.when(core == c)
        def _():
            if ny > 1:
                y_part = outgoing.at[pl.ds(0, ny - 1), :, pl.ds(0, half + 1 - c)]
                pltpu.make_async_copy(y_part, y_part, y_send).wait()
            x_part = across.at[pl.ds(0, half + 1 - c)]
            pltpu.make_async_copy(x_part, x_part, x_send).wait()

    pltpu.make_async_copy(zparts, zparts, z_send).wait()
    pltpu.make_async_copy(gparts, gparts, g_send).wait()
    pltpu.make_async_copy(dparts, dparts, d_send).wait()
    for step in range(ITERS):
        cparts = cbuf.at[step, :, pl.ds(0, (n - 1) * topics)]
        pltpu.make_async_copy(cparts, cparts, c_send.at[step]).wait()
    pltpu.make_async_copy(aparts, aparts, fa_send).wait()


def statistic_kernel(tiles, docs, row, stat, out, weights):
    topics = stat.shape[1]

    @pl.when(pl.program_id(0) == 0)
    def _():
        count = row.shape[0]
        onehot = (
            lax.broadcasted_iota(jnp.int32, (count, docs.shape[1]), 0) == docs[...]
        ).astype(F32).T.astype(BF)
        high, middle = split2(row[...])
        weights[:, :topics] = dot(onehot, high).astype(BF)
        weights[:, topics:] = dot(onehot, middle).astype(BF)

    product = dot(tiles[...], weights[...])
    product = product[:, :topics] + product[:, topics:]
    out[...] = DECAY * stat[...] + product * (1.0 / row.shape[0])


def per_device(n, factor, tile_values, tile_docs, codes, gram_stat, data_stat):
    rows, topics = factor.shape
    width = tile_values.shape[1]
    block = codes.shape[1]
    piece = rows // n
    half = n // 2
    ny = n // 4
    anywhere = pl.BlockSpec(memory_space=pl.ANY)
    vmem = pl.BlockSpec(memory_space=pltpu.VMEM)
    dma = pltpu.SemaphoreType.DMA
    codes_t, row, gram_new = pl.pallas_call(
        functools.partial(codes_kernel, n),
        out_shape=(
            jax.ShapeDtypeStruct((block, topics), F32),
            jax.ShapeDtypeStruct((n * block, topics), F32),
            jax.ShapeDtypeStruct((topics, topics), F32),
        ),
        in_specs=[anywhere, anywhere, vmem, vmem, vmem],
        out_specs=(vmem, vmem, vmem),
        scratch_shapes=[
            pltpu.VMEM((rows, topics), BF),
            pltpu.VMEM((rows, width), BF),
            pltpu.VMEM((n, 2 * piece, topics), BF),
            pltpu.VMEM((n, topics, 2 * piece), BF),
            pltpu.VMEM((2, half + 1, topics, topics), F32),
            pltpu.VMEM((ny, 2, half + 1, topics, topics), BF),
            pltpu.VMEM((ny, 2, half + 1, topics, topics), BF),
            pltpu.VMEM((half + 1, topics, topics), F32),
            pltpu.VMEM((n, topics, topics), F32),
            pltpu.VMEM((n * topics, 2 * topics), BF),
            pltpu.VMEM((topics, 2 * topics), BF),
            pltpu.VMEM((ITERS, 2 * block, n * topics), BF),
            pltpu.VMEM((ITERS, 2 * block, topics), BF),
            pltpu.VMEM((n, block, topics), F32),
            pltpu.VMEM((n, block, topics), F32),
            pltpu.VMEM((block, topics), F32),
            pltpu.VMEM((n, block, topics), F32),
            pltpu.VMEM((n, block, topics), F32),
            dma((2,)), dma, dma((n,)), dma, dma((n,)), dma, dma((ny, 2, half + 1)),
            dma, dma((half + 1,)), dma, dma, dma, dma, dma((ITERS,)), dma((ITERS,)),
            dma, dma, dma, dma, dma, dma,
        ],
        compiler_params=pltpu.CompilerParams(
            collective_id=0, has_side_effects=True, vmem_limit_bytes=48 * 1024 * 1024
        ),
        name="codes",
    )(factor, tile_values, tile_docs, codes.T, gram_stat)
    step = rows // 8
    data_new = pl.pallas_call(
        statistic_kernel,
        grid=(8,),
        out_shape=jax.ShapeDtypeStruct((rows, topics), F32),
        in_specs=[
            pl.BlockSpec((step, width), lambda i: (i, 0)),
            pl.BlockSpec((1, width), lambda i: (0, 0)),
            pl.BlockSpec((n * block, topics), lambda i: (0, 0)),
            pl.BlockSpec((step, topics), lambda i: (i, 0)),
        ],
        out_specs=pl.BlockSpec((step, topics), lambda i: (i, 0)),
        scratch_shapes=[pltpu.VMEM((width, 2 * topics), BF)],
        compiler_params=pltpu.CompilerParams(vmem_limit_bytes=32 * 1024 * 1024),
        name="statistic",
    )(tile_values, tile_docs, row, data_stat)
    return codes_t.T, gram_new, data_new


def solution(mesh):
    placed = (
        P("term", "topic"),
        P("term", None),
        P("term", None),
        P("topic", "term"),
        P("topic", "term"),
        P("term", "topic"),
    )
    return jax.shard_map(
        functools.partial(per_device, mesh.shape["term"]),
        mesh=mesh,
        in_specs=placed,
        out_specs=(P("topic", "term"), P("topic", "term"), P("term", "topic")),
        check_vma=False,
    )
```

```python
import functools

import jax
import jax.numpy as jnp
from jax import lax
from jax.experimental import pallas as pl
from jax.experimental.pallas import tpu as pltpu
from jax.sharding import PartitionSpec as P

ITERS = 3
EPSILON = 1e-06
DECAY = 0.5
MESH = pl.DeviceIdType.MESH
BF = jnp.bfloat16
F32 = jnp.float32


def split2(value):
    high = value.astype(BF)
    return high, (value - high.astype(F32)).astype(BF)


def dot(left, right):
    return jnp.dot(left, right, preferred_element_type=F32)


def codes_kernel(
    n, factor, tiles, docs_in, codes_in, gram_stat_in,
    codes_out, gram_out, weights_out,
    factor_v, tiles_v, docs, codes, gram_stat,
    xx, xt, own, outgoing, incoming, xin, xsum, zin, zsum, tile,
    gcol, gsend, cbuf, csend, dsend, drecv, fsend, arow, brow,
    local_sem, a2a_send, a2a_recv, core_send, core_recv, y_send, y_recv,
    x_send, x_recv, z_send, z_recv, t_send, t_recv, g_send, g_recv, c_send, c_recv,
    d_send, d_recv, fa_send, fa_recv, fb_send, fb_recv,
):
    rows, topics = factor.shape
    piece = rows // n
    block = codes.shape[0]
    half = n // 2
    sets = half + 1
    ny = n // 4
    nz = n // 2
    slim = topics // n
    d = lax.axis_index("term")
    t = lax.axis_index("topic")
    core = d % 2
    xlo = (d // 2) % 2
    y = d // 4
    xhi = t // nz
    z = t % nz
    sibling = d + 1 - 2 * core

    barrier = pltpu.get_barrier_semaphore()

    def greet(s, carry):
        pl.semaphore_signal(barrier, 1, device_id={"topic": (t + s) % n}, device_id_type=MESH)
        pl.semaphore_signal(barrier, 1, device_id={"term": (d + s) % n}, device_id_type=MESH)
        return carry

    lax.fori_loop(1, n, greet, 0)

    def greet_senders(s, carry):
        @pl.when((s != d) | (t != d))
        def _():
            pl.semaphore_signal(barrier, 1, device_id={"term": s, "topic": d}, device_id_type=MESH)
        return carry

    lax.fori_loop(0, n, greet_senders, 0)
    pl.semaphore_signal(
        barrier, 1,
        device_id={"term": y * 4 + (1 - xlo) * 2 + core, "topic": (1 - xhi) * nz + z},
        device_id_type=MESH,
    )
    loads = [
        pltpu.make_async_copy(a, b, local_sem.at[s])
        for s, (a, b) in enumerate(
            [(factor, factor_v), (tiles, tiles_v), (docs_in, docs), (codes_in, codes),
             (gram_stat_in, gram_stat)]
        )
    ]
    load_own = pltpu.make_async_copy(
        factor.at[pl.ds(t * piece, piece)], xx.at[t, pl.ds(core * piece, piece)], a2a_recv.at[t]
    )
    loads[3].start()
    load_own.start()
    for s in (0, 1, 2, 4):
        loads[s].start()

    @pl.when(t == d)
    def _():
        pl.semaphore_wait(barrier, 3 * n - 2)

    @pl.when(t != d)
    def _():
        pl.semaphore_wait(barrier, 3 * n - 1)

    def send_piece(s, carry):
        p = (t + s) % n
        pltpu.make_async_remote_copy(
            factor.at[pl.ds(p * piece, piece)],
            xx.at[t, pl.ds(core * piece, piece)],
            a2a_send,
            a2a_recv.at[t],
            device_id={"topic": p},
            device_id_type=MESH,
        ).start()
        return carry

    lax.fori_loop(1, n, send_piece, 0)

    def share_codes(step, current):
        high, middle = split2(current)
        csend[step, :block, :] = high
        csend[step, block:, :] = middle

        def send_codes(s, carry):
            pltpu.make_async_remote_copy(
                csend.at[step],
                cbuf.at[step, :, pl.ds(pl.multiple_of(t * topics, topics), topics)],
                c_send.at[step],
                c_recv.at[step],
                device_id={"topic": (t + s) % n},
                device_id_type=MESH,
            ).start()
            return carry

        lax.fori_loop(1, n, send_codes, 0)
        cbuf[step, :, pl.ds(pl.multiple_of(t * topics, topics), topics)] = csend[step]

    loads[3].wait()
    share_codes(0, codes[...])

    for s in (0, 1, 2, 4):
        loads[s].wait()
    share = jnp.zeros((tiles.shape[1], topics), F32)
    for s in range(n):
        part = tiles_v[s * piece:(s + 1) * piece, :]
        share = share + lax.dot_general(
            part, factor_v[s * piece:(s + 1) * piece, :], (((0,), (0,)), ((), ())),
            preferred_element_type=F32,
        )
    picks = (
        lax.broadcasted_iota(jnp.int32, (n * block, tiles.shape[1]), 0) == docs[...]
    ).astype(F32)
    onehot = picks.astype(BF)
    high, middle = split2(share)
    low = (share - high.astype(F32) - middle.astype(F32)).astype(BF)
    spread = dot(onehot, high) + dot(onehot, middle) + dot(onehot, low)
    dsend[...] = spread.reshape(n, block, topics)

    def send_share(s, carry):
        target = (d + s) % n
        pltpu.make_async_remote_copy(
            dsend.at[target], drecv.at[d], d_send, d_recv,
            device_id={"term": target}, device_id_type=MESH,
        ).start()
        return carry

    lax.fori_loop(1, n, send_share, 0)
    drecv[d] = dsend[d]

    def place(p, q):
        k = (p + q) % n
        e1 = (p + n - k // 2 - core) % n
        swap = (e1 + half - 1 + core) // n
        i = p + swap * (q - p)
        j = q + swap * (p - q)
        e = (i + n - k // 2 - core) % n
        return k // 4, (k // 2) % 2, e, i, j

    def pair_count(m):
        return (m - (m + core) % 2 + 2) // 2

    def scale_of(y2):
        return 1.0 + ((y2 * 2 + xlo) * n + t).astype(F32) * (1.0 / (2 * ny * n))

    def forward(p):
        return pltpu.make_async_remote_copy(
            xx.at[p, pl.ds(core * piece, piece)],
            xx.at[p, pl.ds(core * piece, piece)],
            core_send,
            core_recv.at[p],
            device_id={"term": sibling},
            device_id_type=MESH,
        )

    scale = scale_of(y)

    def arrive(m):
        p = (t + n - m) % n
        mine = xx.at[p, pl.ds(core * piece, piece)]
        pltpu.make_async_copy(mine, mine, a2a_recv.at[p]).wait()
        forward(p).start()
        theirs = xx.at[p, pl.ds((1 - core) * piece, piece)]
        pltpu.make_async_copy(theirs, theirs, core_recv.at[p]).wait()
        xt[p] = xx[p].T

        def pair(s, carry):
            q = (t + n - ((m + core) % 2 + 2 * s)) % n
            y2, x2, e, i, j = place(p, q)
            product = dot(xt[i], xx[j])

            @pl.when(y2 == y)
            def _():
                own[x2, e] = product

            @pl.when(y2 != y)
            def _():
                outgoing[y2, x2, e] = (product * scale).astype(BF)
                pltpu.make_async_remote_copy(
                    outgoing.at[y2, x2, e], incoming.at[y, x2, e], y_send, y_recv.at[y, x2, e],
                    device_id={"term": y2 * 4 + xlo * 2 + core}, device_id_type=MESH,
                ).start()

            return carry

        lax.fori_loop(0, pair_count(m), pair, 0)

    def reduce_y(m):
        p = (t + n - m) % n

        def pair(s, carry):
            q = (t + n - ((m + core) % 2 + 2 * s)) % n
            y2, x2, e, i, j = place(p, q)

            @pl.when(y2 == y)
            def _():
                total = own[x2, e]
                for r in range(1, ny):
                    y3 = (y + r) % ny
                    got = incoming.at[y3, x2, e]
                    pltpu.make_async_copy(got, got, y_recv.at[y3, x2, e]).wait()
                    total = total + incoming[y3, x2, e].astype(F32) * (1.0 / scale_of(y3))
                own[x2, e] = total
                for h in range(2):
                    @pl.when((x2 != xlo) | (h != xhi))
                    def _():
                        pltpu.make_async_remote_copy(
                            own.at[x2, e, pl.ds(h * (topics // 2), topics // 2)],
                            xin.at[xlo * 2 + xhi, e],
                            x_send,
                            x_recv.at[xlo * 2 + xhi, e],
                            device_id={"term": y * 4 + x2 * 2 + core, "topic": h * nz + z},
                            device_id_type=MESH,
                        ).start()

            return carry

        lax.fori_loop(0, pair_count(m), pair, 0)

    lag = 2

    def first(m, carry):
        arrive(m)
        return carry

    def both(m, carry):
        arrive(m)
        reduce_y(m - lag)
        return carry

    def last(m, carry):
        reduce_y(m)
        return carry

    lax.fori_loop(0, lag, first, 0)
    lax.fori_loop(lag, n, both, 0)
    lax.fori_loop(n - lag, n, last, 0)

    xsum[sets - 1] = jnp.zeros((topics // 2, topics), F32)

    def reduce_x(e, carry):
        total = own[xlo, e, pl.ds(xhi * (topics // 2), topics // 2), :]
        for r in range(1, 4):
            source = (xlo * 2 + xhi + r) % 4
            got = xin.at[source, e]
            pltpu.make_async_copy(got, got, x_recv.at[source, e]).wait()
            total = total + xin[source, e]
        xsum[e] = total
        return carry

    lax.fori_loop(0, sets - core, reduce_x, 0)

    def send_z(s, carry):
        target = (z + s) % nz
        pltpu.make_async_remote_copy(
            xsum.at[:, pl.ds(target * slim, slim)], zin.at[z], z_send, z_recv,
            device_id={"topic": xhi * nz + target}, device_id_type=MESH,
        ).start()
        return carry

    lax.fori_loop(1, nz, send_z, 0)
    zin[z] = xsum[:, pl.ds(z * slim, slim), :]
    zparts = zin.at[pl.ds(0, nz - 1)]
    pltpu.make_async_copy(zparts, zparts, z_recv).wait()
    total = zin[0]
    for s in range(1, nz):
        total = total + zin[s]
    zsum[...] = total

    def send_slim(s, carry):
        target = (t + s) % n
        e1 = (target + n - d // 2 - core) % n
        swap = (e1 + half - 1 + core) // n
        e = e1 + swap * (n - core - 2 * e1)
        pltpu.make_async_remote_copy(
            zsum.at[e], tile.at[pl.ds(t * slim, slim)], t_send, t_recv,
            device_id={"topic": target}, device_id_type=MESH,
        ).start()
        return carry

    lax.fori_loop(1, n, send_slim, 0)
    role = (t + n - d // 2 - core) % n
    swapped = (role + half - 1 + core) // n
    tile[pl.ds(t * slim, slim), :] = zsum[role + swapped * (n - core - 2 * role)]
    tparts = tile.at[pl.ds(0, topics - slim)]
    pltpu.make_async_copy(tparts, tparts, t_recv).wait()

    @pl.when(swapped == 0)
    def _():
        high, middle = split2(tile[...].T)
        gsend[:, :topics] = high
        gsend[:, topics:] = middle

    @pl.when(swapped != 0)
    def _():
        high, middle = split2(tile[...])
        gsend[:, :topics] = high
        gsend[:, topics:] = middle

    def spot(source):
        return pl.ds(((source + n - t) % n) * topics, topics)

    def send_gram(s, carry):
        pltpu.make_async_remote_copy(
            gsend, gcol.at[spot(d)], g_send, g_recv.at[d],
            device_id={"term": (d + 2 * s) % n}, device_id_type=MESH,
        ).start()
        return carry

    lax.fori_loop(1, half, send_gram, 0)
    pltpu.make_async_remote_copy(
        gsend, gcol.at[spot(d)], g_send, g_recv.at[d],
        device_id={"term": sibling}, device_id_type=MESH,
    ).start()
    gcol[spot(d), :] = gsend[...]

    dparts = drecv.at[pl.ds(0, n - 1)]
    pltpu.make_async_copy(dparts, dparts, d_recv).wait()
    data = drecv[0]
    for s in range(1, n):
        data = data + drecv[s]

    def pass_gram(s, carry):
        source = (d + n - 2 * s) % n
        got = gcol.at[spot(source)]
        pltpu.make_async_copy(got, got, g_recv.at[source]).wait()
        pltpu.make_async_remote_copy(
            got, got, g_send, g_recv.at[source],
            device_id={"term": sibling}, device_id_type=MESH,
        ).start()
        return carry

    lax.fori_loop(1, half, pass_gram, 0)

    def take_gram(s, carry):
        source = (sibling + n - 2 * s) % n
        got = gcol.at[spot(source)]
        pltpu.make_async_copy(got, got, g_recv.at[source]).wait()
        return carry

    lax.fori_loop(0, half, take_gram, 0)

    current = codes[...]
    for step in range(ITERS):
        if step > 0:
            share_codes(step, current)
        cparts = cbuf.at[step, :, pl.ds(0, (n - 1) * topics)]
        pltpu.make_async_copy(cparts, cparts, c_recv.at[step]).wait()
        product = dot(cbuf[step], gcol[...])
        applied = product[:, :topics] + product[:, topics:]
        applied = applied[:block] + applied[block:]
        current = current * data / (applied + EPSILON)

    fsend[...] = current

    def send_row(s, carry):
        pltpu.make_async_remote_copy(
            fsend, arow.at[d], fa_send, fa_recv,
            device_id={"term": (d + s) % n}, device_id_type=MESH,
        ).start()
        return carry

    lax.fori_loop(1, n, send_row, 0)

    def send_column(s, carry):
        target = (t + s) % n

        @pl.when((t != d) | (target != t))
        def _():
            pltpu.make_async_remote_copy(
                fsend, brow.at[d], fb_send, fb_recv,
                device_id={"term": t, "topic": target}, device_id_type=MESH,
            ).start()

        return carry

    lax.fori_loop(0, n, send_column, 0)
    codes_out[...] = current
    arow[d] = current
    choose = picks.T.astype(BF)

    sent = factor.at[pl.ds(0, rows - piece)]
    pltpu.make_async_copy(sent, sent, a2a_send).wait()
    pltpu.make_async_copy(factor, factor, core_send).wait()
    for c in range(2):
        @pl.when(core == c)
        def _():
            if ny > 1:
                y_part = outgoing.at[pl.ds(0, ny - 1), :, pl.ds(0, sets - c)]
                pltpu.make_async_copy(y_part, y_part, y_send).wait()
            x_part = xin.at[pl.ds(0, 3), pl.ds(0, sets - c)]
            pltpu.make_async_copy(x_part, x_part, x_send).wait()

    pltpu.make_async_copy(zparts, zparts, z_send).wait()
    pltpu.make_async_copy(tparts, tparts, t_send).wait()
    gparts = gcol.at[pl.ds(0, (n - 1) * topics)]
    pltpu.make_async_copy(gparts, gparts, g_send).wait()
    pltpu.make_async_copy(dparts, dparts, d_send).wait()
    for step in range(ITERS):
        cparts = cbuf.at[step, :, pl.ds(0, (n - 1) * topics)]
        pltpu.make_async_copy(cparts, cparts, c_send.at[step]).wait()

    aparts = arow.at[pl.ds(0, n - 1)]
    pltpu.make_async_copy(aparts, aparts, fa_recv).wait()
    whole = arow[...].reshape(n * block, topics)
    high, middle = split2(whole)
    weights_out[:, :topics] = dot(choose, high).astype(BF)
    weights_out[:, topics:] = dot(choose, middle).astype(BF)
    a_high, a_middle = split2(whole.T)

    @pl.when(t == d)
    def _():
        brow[d] = current
        bparts = brow.at[pl.ds(0, n - 1)]
        pltpu.make_async_copy(bparts, bparts, fb_recv).wait()
        pltpu.make_async_copy(bparts, bparts, fb_send).wait()

    @pl.when(t != d)
    def _():
        pltpu.make_async_copy(brow, brow, fb_recv).wait()
        pltpu.make_async_copy(brow, brow, fb_send).wait()

    b_high, b_middle = split2(brow[...].reshape(n * block, topics))
    outer = dot(a_high, b_high) + (dot(a_high, b_middle) + dot(a_middle, b_high))
    gram_out[...] = DECAY * gram_stat[...] + outer * (1.0 / (n * block))
    pltpu.make_async_copy(aparts, aparts, fa_send).wait()


def statistic_kernel(scale, tiles, weights, stat, codes, gram, out, codes_out, gram_out):
    topics = stat.shape[1]

    @pl.when(pl.program_id(0) == 0)
    def _():
        codes_out[...] = codes[...]
        gram_out[...] = gram[...]

    product = dot(tiles[...], weights[...])
    product = product[:, :topics] + product[:, topics:]
    out[...] = DECAY * stat[...] + product * scale


def per_device(n, factor, tile_values, tile_docs, codes, gram_stat, data_stat):
    rows, topics = factor.shape
    width = tile_values.shape[1]
    block = codes.shape[1]
    piece = rows // n
    sets = n // 2 + 1
    ny = n // 4
    nz = n // 2
    hbm = pl.BlockSpec(memory_space=pltpu.HBM)
    vmem = pl.BlockSpec(memory_space=pltpu.VMEM)
    dma = pltpu.SemaphoreType.DMA
    codes_t, gram, weights = pl.pallas_call(
        functools.partial(codes_kernel, n),
        out_shape=(
            jax.ShapeDtypeStruct((block, topics), F32),
            jax.ShapeDtypeStruct((topics, topics), F32),
            jax.ShapeDtypeStruct((width, 2 * topics), BF),
        ),
        in_specs=[hbm] * 5,
        out_specs=(vmem, vmem, vmem),
        scratch_shapes=[
            pltpu.VMEM((rows, topics), BF),
            pltpu.VMEM((rows, width), BF),
            pltpu.VMEM((1, width), jnp.int32),
            pltpu.VMEM((block, topics), F32),
            pltpu.VMEM((topics, topics), F32),
            pltpu.VMEM((n, 2 * piece, topics), BF),
            pltpu.VMEM((n, topics, 2 * piece), BF),
            pltpu.VMEM((2, sets, topics, topics), F32),
            pltpu.VMEM((ny, 2, sets, topics, topics), BF),
            pltpu.VMEM((ny, 2, sets, topics, topics), BF),
            pltpu.VMEM((4, sets, topics // 2, topics), F32),
            pltpu.VMEM((sets, topics // 2, topics), F32),
            pltpu.VMEM((nz, sets, topics // n, topics), F32),
            pltpu.VMEM((sets, topics // n, topics), F32),
            pltpu.VMEM((topics, topics), F32),
            pltpu.VMEM((n * topics, 2 * topics), BF),
            pltpu.VMEM((topics, 2 * topics), BF),
            pltpu.VMEM((ITERS, 2 * block, n * topics), BF),
            pltpu.VMEM((ITERS, 2 * block, topics), BF),
            pltpu.VMEM((n, block, topics), F32),
            pltpu.VMEM((n, block, topics), F32),
            pltpu.VMEM((block, topics), F32),
            pltpu.VMEM((n, block, topics), F32),
            pltpu.VMEM((n, block, topics), F32),
            dma((5,)), dma, dma((n,)), dma, dma((n,)), dma, dma((ny, 2, sets)),
            dma, dma((4, sets)), dma, dma, dma, dma, dma, dma((n,)), dma((ITERS,)), dma((ITERS,)),
            dma, dma, dma, dma, dma, dma,
        ],
        compiler_params=pltpu.CompilerParams(
            collective_id=0, has_side_effects=True, vmem_limit_bytes=62 * 1024 * 1024
        ),
        name="codes",
    )(factor, tile_values, tile_docs, codes.T, gram_stat)
    step = rows // 8
    whole = lambda i: (0, 0)
    part = lambda i: (i, 0)
    data_new, codes_new, gram_new = pl.pallas_call(
        functools.partial(statistic_kernel, 1.0 / (n * block)),
        grid=(8,),
        out_shape=(
            jax.ShapeDtypeStruct((rows, topics), F32),
            jax.ShapeDtypeStruct((block, topics), F32),
            jax.ShapeDtypeStruct((topics, topics), F32),
        ),
        in_specs=[
            pl.BlockSpec((step, width), part),
            pl.BlockSpec((width, 2 * topics), whole),
            pl.BlockSpec((step, topics), part),
            pl.BlockSpec((block, topics), whole),
            pl.BlockSpec((topics, topics), whole),
        ],
        out_specs=(
            pl.BlockSpec((step, topics), part),
            pl.BlockSpec((block, topics), whole),
            pl.BlockSpec((topics, topics), whole),
        ),
        compiler_params=pltpu.CompilerParams(vmem_limit_bytes=62 * 1024 * 1024),
        name="statistic",
    )(tile_values, weights, data_stat, codes_t, gram)
    return codes_new.T, gram_new, data_new


def solution(mesh):
    placed = (
        P("term", "topic"),
        P("term", None),
        P("term", None),
        P("topic", "term"),
        P("topic", "term"),
        P("term", "topic"),
    )
    return jax.shard_map(
        functools.partial(per_device, mesh.shape["term"]),
        mesh=mesh,
        in_specs=placed,
        out_specs=(P("topic", "term"), P("topic", "term"), P("term", "topic")),
        check_vma=False,
    )
```

```python
import functools

import jax
import jax.numpy as jnp
from jax import lax
from jax.experimental import pallas as pl
from jax.experimental.pallas import tpu as pltpu
from jax.sharding import PartitionSpec as P

ITERS = 3
EPSILON = 1e-06
DECAY = 0.5
LAG_Y = 2
LAG_X = 4
HOLD = 11
MESH = pl.DeviceIdType.MESH
BF = jnp.bfloat16
F32 = jnp.float32


def split2(value):
    high = value.astype(BF)
    return high, (value - high.astype(F32)).astype(BF)


def rem(value, count):
    return lax.rem(value, jnp.int32(count))


def quo(value, count):
    return lax.div(value, jnp.int32(count))


def dot(left, right):
    return jnp.dot(left, right, preferred_element_type=F32)


def codes_kernel(
    n, factor, tiles, docs_in, codes_in, gram_stat_in,
    codes_out, gram_out, weights_out,
    factor_v, tiles_v, docs, codes, gram_stat,
    xx, xt, product, own, outgoing, incoming, xin, xsum, zin, zsum, tile,
    gcol, gsend, cbuf, csend, dsend, drecv, fsend, arow, brow,
    local_sem, a2a_send, a2a_recv, core_send, core_recv, y_send, y_recv,
    x_send, x_recv, z_send, z_recv, t_send, t_recv, g_send, g_recv, c_send, c_recv,
    d_send, d_recv, fa_send, fa_recv, fb_send, fb_recv,
):
    rows, topics = factor.shape
    width = tiles.shape[1]
    piece = rows // n
    block = codes.shape[0]
    half = n // 2
    sets = half + 1
    group = min(4, half)
    ny = n // 4
    nz = n // 2
    slim = topics // n
    d = lax.axis_index("term")
    t = lax.axis_index("topic")
    core = rem(d, 2)
    xlo = rem(quo(d, 2), 2)
    y = quo(d, 4)
    xhi = quo(t, nz)
    z = rem(t, nz)
    sibling = d + 1 - 2 * core

    barrier = pltpu.get_barrier_semaphore()

    def greet(s, carry):
        pl.semaphore_signal(barrier, 1, device_id={"topic": rem(t + s, n)}, device_id_type=MESH)
        pl.semaphore_signal(barrier, 1, device_id={"term": rem(d + s, n)}, device_id_type=MESH)
        return carry

    lax.fori_loop(1, n, greet, 0)

    def greet_senders(s, carry):
        @pl.when((s != d) | (t != d))
        def _():
            pl.semaphore_signal(barrier, 1, device_id={"term": s, "topic": d}, device_id_type=MESH)
        return carry

    lax.fori_loop(0, n, greet_senders, 0)
    pl.semaphore_signal(
        barrier, 1,
        device_id={"term": y * 4 + (1 - xlo) * 2 + core, "topic": (1 - xhi) * nz + z},
        device_id_type=MESH,
    )
    loads = [
        pltpu.make_async_copy(a, b, local_sem.at[s])
        for s, (a, b) in enumerate(
            [(factor, factor_v), (tiles, tiles_v), (docs_in, docs), (codes_in, codes),
             (gram_stat_in, gram_stat)]
        )
    ]
    load_own = pltpu.make_async_copy(
        factor.at[pl.ds(t * piece, piece)], xx.at[t, pl.ds(core * piece, piece)], a2a_recv.at[t]
    )
    loads[3].start()
    load_own.start()
    for s in (0, 1, 2, 4):
        loads[s].start()

    @pl.when(t == d)
    def _():
        pl.semaphore_wait(barrier, 3 * n - 2)

    @pl.when(t != d)
    def _():
        pl.semaphore_wait(barrier, 3 * n - 1)

    def piece_at(m):
        u = quo(m, 2)
        odd = rem(u, 2)
        offset = odd * quo(u + 1, 2) + (1 - odd) * (nz - quo(u, 2))
        return rem(m, 2) * nz + rem(z + offset, nz)

    def send_piece(s, carry):
        p = piece_at(s)

        @pl.when(p != t)
        def _():
            pltpu.make_async_remote_copy(
                factor.at[pl.ds(p * piece, piece)],
                xx.at[t, pl.ds(core * piece, piece)],
                a2a_send,
                a2a_recv.at[t],
                device_id={"topic": p},
                device_id_type=MESH,
            ).start()

        return carry

    lax.fori_loop(0, n - 2, send_piece, 0)

    def share_codes(step, current):
        high, middle = split2(current)
        csend[step, :block, :] = high
        csend[step, block:, :] = middle

        def send_codes(s, carry):
            pltpu.make_async_remote_copy(
                csend.at[step],
                cbuf.at[step, :, pl.ds(pl.multiple_of(t * topics, topics), topics)],
                c_send.at[step],
                c_recv.at[step],
                device_id={"topic": rem(t + s, n)},
                device_id_type=MESH,
            ).start()
            return carry

        lax.fori_loop(1, n, send_codes, 0)
        cbuf[step, :, pl.ds(pl.multiple_of(t * topics, topics), topics)] = csend[step]


    for load in loads:
        load.wait()
    share = jnp.zeros((tiles.shape[1], topics), F32)
    for s in range(n):
        part = tiles_v[s * piece:(s + 1) * piece, :]
        share = share + lax.dot_general(
            part, factor_v[s * piece:(s + 1) * piece, :], (((0,), (0,)), ((), ())),
            preferred_element_type=F32,
        )
    picks = (
        lax.broadcasted_iota(jnp.int32, (n * block, tiles.shape[1]), 0) == docs[...]
    ).astype(F32)
    onehot = picks.astype(BF)
    high, middle = split2(share)
    low = (share - high.astype(F32) - middle.astype(F32)).astype(BF)
    spread = dot(onehot, high) + dot(onehot, middle) + dot(onehot, low)
    dsend[...] = spread.reshape(n, block, topics)

    def send_share(s, carry):
        target = rem(d + s, n)
        pltpu.make_async_remote_copy(
            dsend.at[target], drecv.at[d], d_send, d_recv,
            device_id={"term": target}, device_id_type=MESH,
        ).start()
        return carry

    lax.fori_loop(1, n, send_share, 0)
    drecv[d] = dsend[d]

    def place(p, q):
        k = rem(p + q, n)
        k_half = quo(k, 2)
        e1 = rem(p + n - k_half - core, n)
        swap = quo(e1 + half - 1 + core, n)
        e = e1 + swap * (n - core - 2 * e1)
        return quo(k_half, 2), rem(k_half, 2), e, swap

    def side_of(m):
        return rem(quo(quo(m, 2) + 1, 2), 2)

    def pair_count(m):
        u = quo(m, 2)
        return core * 2 * quo(u + 1, 2) + (1 - core) * (2 * quo(u, 2) + rem(m, 2) + 1)

    def partner(side, s):
        rank = quo(s, 2)
        return piece_at(4 * rank + 2 * rem(rank + side, 2) + rem(s, 2))

    def scale_of(y2):
        return 1.0 + ((y2 * 2 + xlo) * n + t).astype(F32) * (1.0 / (2 * ny * n))

    scale = scale_of(y)
    unscale = [1.0 / scale_of(rem(y + r, ny)) for r in range(ny)]
    xsum[sets - 1] = jnp.zeros((topics // 2, topics), F32)

    def arrive(m):
        p = piece_at(m)
        mine = xx.at[p, pl.ds(core * piece, piece)]
        theirs = xx.at[p, pl.ds((1 - core) * piece, piece)]
        pltpu.make_async_copy(mine, mine, a2a_recv.at[p]).wait()
        pltpu.make_async_remote_copy(
            mine, mine, core_send, core_recv.at[p],
            device_id={"term": sibling}, device_id_type=MESH,
        ).start()

        @pl.when(m == min(HOLD, n - 3))
        def _():
            lax.fori_loop(n - 2, n, send_piece, 0)

        pltpu.make_async_copy(theirs, theirs, core_recv.at[p]).wait()
        xt[side_of(m), 2 * quo(m, 4) + rem(m, 2)] = xx[p].T
        side = rem(side_of(m) + core, 2)
        count = pair_count(m)

        def multiply(g, carry):
            left = xt[side, pl.ds(g * group, group)].reshape(group * topics, 2 * piece)
            product[pl.ds(g * group, group)] = dot(left, xx[p]).reshape(group, topics, topics)
            return carry

        lax.fori_loop(0, quo(count + group - 1, group), multiply, 0)

        def pair(s, carry):
            y2, x2, e, swap = place(p, partner(side, s))

            @pl.when(swap == 0)
            def _():
                product[s] = product[s].T

            @pl.when(y2 == y)
            def _():
                own[x2, e] = product[s]

            @pl.when(y2 != y)
            def _():
                outgoing[y2, x2, e] = (product[s] * scale).astype(BF)
                pltpu.make_async_remote_copy(
                    outgoing.at[y2, x2, e], incoming.at[y, x2, e], y_send, y_recv.at[y, x2, e],
                    device_id={"term": y2 * 4 + xlo * 2 + core}, device_id_type=MESH,
                ).start()

            return carry

        lax.fori_loop(0, count, pair, 0)

    def walk(m, body):
        p = piece_at(m)
        side = rem(side_of(m) + core, 2)

        def pair(s, carry):
            y2, x2, e, swap = place(p, partner(side, s))
            body(y2, x2, e)
            return carry

        lax.fori_loop(0, pair_count(m), pair, 0)

    def reduce_y(y2, x2, e):
        @pl.when(y2 == y)
        def _():
            total = own[x2, e]
            for r in range(1, ny):
                y3 = rem(y + r, ny)
                got = incoming.at[y3, x2, e]
                pltpu.make_async_copy(got, got, y_recv.at[y3, x2, e]).wait()
                total = total + incoming[y3, x2, e].astype(F32) * unscale[r]
            own[x2, e] = total
            for h in range(2):
                @pl.when((x2 != xlo) | (h != xhi))
                def _():
                    pltpu.make_async_remote_copy(
                        own.at[x2, e, pl.ds(h * (topics // 2), topics // 2)],
                        xin.at[xlo * 2 + xhi, e],
                        x_send,
                        x_recv.at[xlo * 2 + xhi, e],
                        device_id={"term": y * 4 + x2 * 2 + core, "topic": h * nz + z},
                        device_id_type=MESH,
                    ).start()

    def reduce_x(y2, x2, e):
        @pl.when((y2 == y) & (x2 == xlo))
        def _():
            total = own[xlo, e, pl.ds(xhi * (topics // 2), topics // 2), :]
            for r in range(1, 4):
                source = rem(xlo * 2 + xhi + r, 4)
                got = xin.at[source, e]
                pltpu.make_async_copy(got, got, x_recv.at[source, e]).wait()
                total = total + xin[source, e]
            xsum[e] = total
            send_z(e)

    def send_z(e):
        def send(s, carry):
            target = rem(z + s, nz)
            pltpu.make_async_remote_copy(
                xsum.at[e, pl.ds(target * slim, slim)], zin.at[z, e], z_send, z_recv,
                device_id={"topic": xhi * nz + target}, device_id_type=MESH,
            ).start()
            return carry

        lax.fori_loop(1, nz, send, 0)

    @pl.when(core == 1)
    def _():
        send_z(sets - 1)

    def steps(start, stop, first_lag, second_lag):
        def step(m, carry):
            if first_lag >= 0:
                arrive(m)
            if second_lag >= 1:
                walk(m - LAG_Y, reduce_y)
            if second_lag >= 2:
                walk(m - LAG_X, reduce_x)
            return carry

        lax.fori_loop(start, stop, step, 0)

    steps(0, LAG_Y, 0, 0)
    steps(LAG_Y, min(LAG_X, n), 0, 1)
    steps(LAG_X, n, 0, 2)
    share_codes(0, codes[...])
    steps(n, n + LAG_Y, -1, 2)

    def drain(m, carry):
        walk(m, reduce_x)
        return carry

    lax.fori_loop(n + LAG_Y - LAG_X, n, drain, 0)

    zin[z] = xsum[:, pl.ds(z * slim, slim), :]
    zparts = zin.at[pl.ds(0, nz - 1)]
    pltpu.make_async_copy(zparts, zparts, z_recv).wait()
    total = zin[0]
    for s in range(1, nz):
        total = total + zin[s]
    zsum[...] = total

    def send_slim(s, carry):
        target = rem(t + s, n)
        e1 = rem(target + n - quo(d, 2) - core, n)
        swap = quo(e1 + half - 1 + core, n)
        e = e1 + swap * (n - core - 2 * e1)
        pltpu.make_async_remote_copy(
            zsum.at[e], tile.at[pl.ds(t * slim, slim)], t_send, t_recv,
            device_id={"topic": target}, device_id_type=MESH,
        ).start()
        return carry

    lax.fori_loop(1, n, send_slim, 0)
    role = rem(t + n - quo(d, 2) - core, n)
    swapped = quo(role + half - 1 + core, n)
    tile[pl.ds(t * slim, slim), :] = zsum[role + swapped * (n - core - 2 * role)]
    tparts = tile.at[pl.ds(0, topics - slim)]
    pltpu.make_async_copy(tparts, tparts, t_recv).wait()

    @pl.when(swapped == 0)
    def _():
        high, middle = split2(tile[...].T)
        gsend[:, :topics] = high
        gsend[:, topics:] = middle

    @pl.when(swapped != 0)
    def _():
        high, middle = split2(tile[...])
        gsend[:, :topics] = high
        gsend[:, topics:] = middle

    def spot(source):
        return pl.ds(rem(source + n - t, n) * topics, topics)

    def send_gram(s, carry):
        pltpu.make_async_remote_copy(
            gsend, gcol.at[spot(d)], g_send, g_recv.at[d],
            device_id={"term": rem(d + 2 * s, n)}, device_id_type=MESH,
        ).start()
        return carry

    lax.fori_loop(1, half, send_gram, 0)
    pltpu.make_async_remote_copy(
        gsend, gcol.at[spot(d)], g_send, g_recv.at[d],
        device_id={"term": sibling}, device_id_type=MESH,
    ).start()
    gcol[spot(d), :] = gsend[...]

    dparts = drecv.at[pl.ds(0, n - 1)]
    pltpu.make_async_copy(dparts, dparts, d_recv).wait()
    data = drecv[0]
    for s in range(1, n):
        data = data + drecv[s]

    def pass_gram(s, carry):
        source = rem(d + n - 2 * s, n)
        got = gcol.at[spot(source)]
        pltpu.make_async_copy(got, got, g_recv.at[source]).wait()
        pltpu.make_async_remote_copy(
            got, got, g_send, g_recv.at[source],
            device_id={"term": sibling}, device_id_type=MESH,
        ).start()
        return carry

    lax.fori_loop(1, half, pass_gram, 0)

    def take_gram(s, carry):
        source = rem(sibling + n - 2 * s, n)
        got = gcol.at[spot(source)]
        pltpu.make_async_copy(got, got, g_recv.at[source]).wait()
        return carry

    lax.fori_loop(0, half, take_gram, 0)

    current = codes[...]
    for step in range(ITERS):
        if step > 0:
            share_codes(step, current)
        cparts = cbuf.at[step, :, pl.ds(0, (n - 1) * topics)]
        pltpu.make_async_copy(cparts, cparts, c_recv.at[step]).wait()
        applied = dot(cbuf[step], gcol[...])
        applied = applied[:, :topics] + applied[:, topics:]
        applied = applied[:block] + applied[block:]
        current = current * data / (applied + EPSILON)

    fsend[...] = current

    def send_row(s, carry):
        pltpu.make_async_remote_copy(
            fsend, arow.at[d], fa_send, fa_recv,
            device_id={"term": rem(d + s, n)}, device_id_type=MESH,
        ).start()
        return carry

    lax.fori_loop(1, n, send_row, 0)

    def send_column(s, carry):
        target = rem(t + s, n)

        @pl.when((t != d) | (target != t))
        def _():
            pltpu.make_async_remote_copy(
                fsend, brow.at[d], fb_send, fb_recv,
                device_id={"term": t, "topic": target}, device_id_type=MESH,
            ).start()

        return carry

    lax.fori_loop(0, n, send_column, 0)
    codes_out[...] = current
    arow[d] = current
    choose = picks.T.astype(BF)

    sent = factor.at[pl.ds(0, rows - piece)]
    pltpu.make_async_copy(sent, sent, a2a_send).wait()
    pltpu.make_async_copy(factor, factor, core_send).wait()
    for c in range(2):
        @pl.when(core == c)
        def _():
            if ny > 1:
                y_part = outgoing.at[pl.ds(0, ny - 1), :, pl.ds(0, sets - c)]
                pltpu.make_async_copy(y_part, y_part, y_send).wait()
            x_part = xin.at[pl.ds(0, 3), pl.ds(0, sets - c)]
            pltpu.make_async_copy(x_part, x_part, x_send).wait()

    pltpu.make_async_copy(zparts, zparts, z_send).wait()
    pltpu.make_async_copy(tparts, tparts, t_send).wait()
    gparts = gcol.at[pl.ds(0, (n - 1) * topics)]
    pltpu.make_async_copy(gparts, gparts, g_send).wait()
    pltpu.make_async_copy(dparts, dparts, d_send).wait()
    for step in range(ITERS):
        cparts = cbuf.at[step, :, pl.ds(0, (n - 1) * topics)]
        pltpu.make_async_copy(cparts, cparts, c_send.at[step]).wait()

    aparts = arow.at[pl.ds(0, n - 1)]
    pltpu.make_async_copy(aparts, aparts, fa_recv).wait()
    whole = arow[...].reshape(n * block, topics)
    high, middle = split2(whole)
    share_of_one = 1.0 / (n * block)
    weights_out[:width, :] = (dot(choose, high) * share_of_one).astype(BF)
    weights_out[width:, :] = (dot(choose, middle) * share_of_one).astype(BF)
    a_high, a_middle = split2(whole.T)

    @pl.when(t == d)
    def _():
        brow[d] = current
        bparts = brow.at[pl.ds(0, n - 1)]
        pltpu.make_async_copy(bparts, bparts, fb_recv).wait()
        pltpu.make_async_copy(bparts, bparts, fb_send).wait()

    @pl.when(t != d)
    def _():
        pltpu.make_async_copy(brow, brow, fb_recv).wait()
        pltpu.make_async_copy(brow, brow, fb_send).wait()

    b_high, b_middle = split2(brow[...].reshape(n * block, topics))
    outer = dot(a_high, b_high) + (dot(a_high, b_middle) + dot(a_middle, b_high))
    gram_out[...] = DECAY * gram_stat[...] + outer * (1.0 / (n * block))
    pltpu.make_async_copy(aparts, aparts, fa_send).wait()


def statistic_kernel(tiles, weights, stat, codes, gram, out, codes_out, gram_out):
    @pl.when(pl.program_id(0) == 0)
    def _():
        codes_out[...] = codes[...]
        gram_out[...] = gram[...]

    part = tiles[...]
    out[...] = DECAY * stat[...] + dot(jnp.concatenate([part, part], axis=1), weights[...])


def per_device(n, factor, tile_values, tile_docs, codes, gram_stat, data_stat):
    rows, topics = factor.shape
    width = tile_values.shape[1]
    block = codes.shape[1]
    piece = rows // n
    sets = n // 2 + 1
    ny = n // 4
    nz = n // 2
    hbm = pl.BlockSpec(memory_space=pltpu.HBM)
    vmem = pl.BlockSpec(memory_space=pltpu.VMEM)
    dma = pltpu.SemaphoreType.DMA
    codes_t, gram, weights = pl.pallas_call(
        functools.partial(codes_kernel, n),
        out_shape=(
            jax.ShapeDtypeStruct((block, topics), F32),
            jax.ShapeDtypeStruct((topics, topics), F32),
            jax.ShapeDtypeStruct((2 * width, topics), BF),
        ),
        in_specs=[hbm] * 5,
        out_specs=(vmem, vmem, vmem),
        scratch_shapes=[
            pltpu.VMEM((rows, topics), BF),
            pltpu.VMEM((rows, width), BF),
            pltpu.VMEM((1, width), jnp.int32),
            pltpu.VMEM((block, topics), F32),
            pltpu.VMEM((topics, topics), F32),
            pltpu.VMEM((n, 2 * piece, topics), BF),
            pltpu.VMEM((2, n // 2, topics, 2 * piece), BF),
            pltpu.VMEM((n // 2, topics, topics), F32),
            pltpu.VMEM((2, sets, topics, topics), F32),
            pltpu.VMEM((ny, 2, sets, topics, topics), BF),
            pltpu.VMEM((ny, 2, sets, topics, topics), BF),
            pltpu.VMEM((4, sets, topics // 2, topics), F32),
            pltpu.VMEM((sets, topics // 2, topics), F32),
            pltpu.VMEM((nz, sets, topics // n, topics), F32),
            pltpu.VMEM((sets, topics // n, topics), F32),
            pltpu.VMEM((topics, topics), F32),
            pltpu.VMEM((n * topics, 2 * topics), BF),
            pltpu.VMEM((topics, 2 * topics), BF),
            pltpu.VMEM((ITERS, 2 * block, n * topics), BF),
            pltpu.VMEM((ITERS, 2 * block, topics), BF),
            pltpu.VMEM((n, block, topics), F32),
            pltpu.VMEM((n, block, topics), F32),
            pltpu.VMEM((block, topics), F32),
            pltpu.VMEM((n, block, topics), F32),
            pltpu.VMEM((n, block, topics), F32),
            dma((5,)), dma, dma((n,)), dma, dma((n,)), dma, dma((ny, 2, sets)),
            dma, dma((4, sets)), dma, dma, dma, dma, dma, dma((n,)), dma((ITERS,)), dma((ITERS,)),
            dma, dma, dma, dma, dma, dma,
        ],
        compiler_params=pltpu.CompilerParams(
            collective_id=0, has_side_effects=True, vmem_limit_bytes=62 * 1024 * 1024
        ),
        name="codes",
    )(factor, tile_values, tile_docs, codes.T, gram_stat)
    step = rows // 8
    whole = lambda i: (0, 0)
    part = lambda i: (i, 0)
    data_new, codes_new, gram_new = pl.pallas_call(
        statistic_kernel,
        grid=(8,),
        out_shape=(
            jax.ShapeDtypeStruct((rows, topics), F32),
            jax.ShapeDtypeStruct((block, topics), F32),
            jax.ShapeDtypeStruct((topics, topics), F32),
        ),
        in_specs=[
            pl.BlockSpec((step, width), part),
            pl.BlockSpec((2 * width, topics), whole),
            pl.BlockSpec((step, topics), part),
            pl.BlockSpec((block, topics), whole),
            pl.BlockSpec((topics, topics), whole),
        ],
        out_specs=(
            pl.BlockSpec((step, topics), part),
            pl.BlockSpec((block, topics), whole),
            pl.BlockSpec((topics, topics), whole),
        ),
        compiler_params=pltpu.CompilerParams(vmem_limit_bytes=62 * 1024 * 1024),
        name="statistic",
    )(tile_values, weights, data_stat, codes_t, gram)
    return codes_new.T, gram_new, data_new


def solution(mesh):
    placed = (
        P("term", "topic"),
        P("term", None),
        P("term", None),
        P("topic", "term"),
        P("topic", "term"),
        P("term", "topic"),
    )
    return jax.shard_map(
        functools.partial(per_device, mesh.shape["term"]),
        mesh=mesh,
        in_specs=placed,
        out_specs=(P("topic", "term"), P("topic", "term"), P("term", "topic")),
        check_vma=False,
    )
```

```python
import functools

import jax
import jax.numpy as jnp
from jax import lax
from jax.experimental import pallas as pl
from jax.experimental.pallas import tpu as pltpu
from jax.sharding import PartitionSpec as P

ITERS = 3
EPSILON = 1e-06
DECAY = 0.5
PARTS = 4
LAG_Y = 3
LAG_X = 6
HOLD = 10
MESH = pl.DeviceIdType.MESH
BF = jnp.bfloat16
F32 = jnp.float32


def split2(value):
    high = value.astype(BF)
    return high, (value - high.astype(F32)).astype(BF)


def rem(value, count):
    return lax.rem(value, jnp.int32(count))


def quo(value, count):
    return lax.div(value, jnp.int32(count))


def dot(left, right):
    return jnp.dot(left, right, preferred_element_type=F32)


def codes_kernel(
    n, factor, tiles, docs_in, codes_in, gram_stat_in,
    codes_out, gram_out, weights_out,
    factor_v, tiles_v, docs, codes, gram_stat,
    xx, xt, product, own, outgoing, incoming, xin, xsum, zin, zsum, tile,
    gcol, gsend, cbuf, csend, dsend, drecv, fsend, arow, brow,
    local_sem, a2a_send, a2a_recv, core_send, core_recv, y_send, y_recv,
    x_send, x_recv, z_send, z_recv, t_send, t_recv, g_send, g_recv, c_send, c_recv,
    d_send, d_recv, fa_send, fa_recv, fb_send, fb_recv,
):
    rows, topics = factor.shape
    width = tiles.shape[1]
    piece = rows // n
    block = codes.shape[0]
    half = n // 2
    sets = half + 1
    group = min(4, half)
    ny = n // 4
    nz = n // 2
    slim = topics // n
    d = lax.axis_index("term")
    t = lax.axis_index("topic")
    core = rem(d, 2)
    xlo = rem(quo(d, 2), 2)
    y = quo(d, 4)
    xhi = quo(t, nz)
    z = rem(t, nz)
    sibling = d + 1 - 2 * core

    barrier = pltpu.get_barrier_semaphore()

    def greet(s, carry):
        pl.semaphore_signal(barrier, 1, device_id={"topic": rem(t + s, n)}, device_id_type=MESH)
        pl.semaphore_signal(barrier, 1, device_id={"term": rem(d + s, n)}, device_id_type=MESH)
        return carry

    lax.fori_loop(1, n, greet, 0)

    def greet_senders(s, carry):
        @pl.when((s != d) | (t != d))
        def _():
            pl.semaphore_signal(barrier, 1, device_id={"term": s, "topic": d}, device_id_type=MESH)
        return carry

    lax.fori_loop(0, n, greet_senders, 0)
    pl.semaphore_signal(
        barrier, 1,
        device_id={"term": y * 4 + (1 - xlo) * 2 + core, "topic": (1 - xhi) * nz + z},
        device_id_type=MESH,
    )
    loads = [
        pltpu.make_async_copy(a, b, local_sem.at[s])
        for s, (a, b) in enumerate(
            [(factor, factor_v), (tiles, tiles_v), (docs_in, docs), (codes_in, codes),
             (gram_stat_in, gram_stat)]
        )
    ]
    load_own = pltpu.make_async_copy(
        factor.at[pl.ds(t * piece, piece)], xx.at[t, pl.ds(core * piece, piece)], a2a_recv.at[t]
    )
    loads[3].start()
    load_own.start()
    for s in (0, 1, 2, 4):
        loads[s].start()

    @pl.when(t == d)
    def _():
        pl.semaphore_wait(barrier, 3 * n - 2)

    @pl.when(t != d)
    def _():
        pl.semaphore_wait(barrier, 3 * n - 1)

    def piece_at(m):
        u = quo(m, 2)
        odd = rem(u, 2)
        offset = odd * quo(u + 1, 2) + (1 - odd) * (nz - quo(u, 2))
        return rem(m, 2) * nz + rem(z + offset, nz)

    def send_piece(s, carry):
        p = piece_at(s)

        @pl.when(p != t)
        def _():
            pltpu.make_async_remote_copy(
                factor.at[pl.ds(p * piece, piece)],
                xx.at[t, pl.ds(core * piece, piece)],
                a2a_send,
                a2a_recv.at[t],
                device_id={"topic": p},
                device_id_type=MESH,
            ).start()

        return carry

    lax.fori_loop(0, n - 2, send_piece, 0)

    def share_codes(step, current):
        high, middle = split2(current)
        csend[step, :block, :] = high
        csend[step, block:, :] = middle

        def send_codes(s, carry):
            target = piece_at(n - 1 - s)

            @pl.when(target != t)
            def _():
                pltpu.make_async_remote_copy(
                    csend.at[step],
                    cbuf.at[step, :, pl.ds(pl.multiple_of(t * topics, topics), topics)],
                    c_send.at[step],
                    c_recv.at[step],
                    device_id={"topic": target},
                    device_id_type=MESH,
                ).start()

            return carry

        lax.fori_loop(0, n, send_codes, 0)
        cbuf[step, :, pl.ds(pl.multiple_of(t * topics, topics), topics)] = csend[step]


    for load in loads:
        load.wait()
    share = jnp.zeros((tiles.shape[1], topics), F32)
    for s in range(n):
        part = tiles_v[s * piece:(s + 1) * piece, :]
        share = share + lax.dot_general(
            part, factor_v[s * piece:(s + 1) * piece, :], (((0,), (0,)), ((), ())),
            preferred_element_type=F32,
        )
    picks = (
        lax.broadcasted_iota(jnp.int32, (n * block, tiles.shape[1]), 0) == docs[...]
    ).astype(F32)
    onehot = picks.astype(BF)
    high, middle = split2(share)
    low = (share - high.astype(F32) - middle.astype(F32)).astype(BF)
    spread = dot(onehot, high) + dot(onehot, middle) + dot(onehot, low)
    dsend[...] = spread.reshape(n, block, topics)

    def send_share(s, carry):
        target = rem(d + s, n)
        pltpu.make_async_remote_copy(
            dsend.at[target], drecv.at[d], d_send, d_recv,
            device_id={"term": target}, device_id_type=MESH,
        ).start()
        return carry

    lax.fori_loop(1, n, send_share, 0)
    drecv[d] = dsend[d]

    def place(p, q):
        k = rem(p + q, n)
        k_half = quo(k, 2)
        e1 = rem(p + n - k_half - core, n)
        swap = quo(e1 + half - 1 + core, n)
        e = e1 + swap * (n - core - 2 * e1)
        return quo(k_half, 2), rem(k_half, 2), e, swap

    def side_of(m):
        return rem(quo(quo(m, 2) + 1, 2), 2)

    def pair_count(m):
        u = quo(m, 2)
        return core * 2 * quo(u + 1, 2) + (1 - core) * (2 * quo(u, 2) + rem(m, 2) + 1)

    def partner(side, s):
        rank = quo(s, 2)
        return piece_at(4 * rank + 2 * rem(rank + side, 2) + rem(s, 2))

    def scale_of(y2):
        return 1.0 + ((y2 * 2 + xlo) * n + t).astype(F32) * (1.0 / (2 * ny * n))

    scale = scale_of(y)
    unscale = [1.0 / scale_of(rem(y + r, ny)) for r in range(ny)]
    xsum[sets - 1] = jnp.zeros((topics // 2, topics), F32)

    def arrive(m):
        p = piece_at(m)
        mine = xx.at[p, pl.ds(core * piece, piece)]
        theirs = xx.at[p, pl.ds((1 - core) * piece, piece)]
        pltpu.make_async_copy(mine, mine, a2a_recv.at[p]).wait()
        pltpu.make_async_remote_copy(
            mine, mine, core_send, core_recv.at[p],
            device_id={"term": sibling}, device_id_type=MESH,
        ).start()

        @pl.when(m == min(HOLD, n - 3))
        def _():
            lax.fori_loop(n - 2, n, send_piece, 0)

        pltpu.make_async_copy(theirs, theirs, core_recv.at[p]).wait()
        xt[side_of(m), 2 * quo(m, 4) + rem(m, 2)] = xx[p].T
        side = rem(side_of(m) + core, 2)
        count = pair_count(m)

        def multiply(g, carry):
            left = xt[side, pl.ds(g * group, group)].reshape(group * topics, 2 * piece)
            product[pl.ds(g * group, group)] = dot(left, xx[p]).reshape(group, topics, topics)
            return carry

        lax.fori_loop(0, quo(count + group - 1, group), multiply, 0)

        def pair(s, carry):
            y2, x2, e, swap = place(p, partner(side, s))

            @pl.when(swap == 0)
            def _():
                product[s] = product[s].T

            @pl.when(y2 == y)
            def _():
                own[x2, e] = product[s]

            @pl.when(y2 != y)
            def _():
                outgoing[y2, x2, e] = (product[s] * scale).astype(BF)
                pltpu.make_async_remote_copy(
                    outgoing.at[y2, x2, e], incoming.at[y, x2, e], y_send, y_recv.at[y, x2, e],
                    device_id={"term": y2 * 4 + xlo * 2 + core}, device_id_type=MESH,
                ).start()

            return carry

        lax.fori_loop(0, count, pair, 0)

    def walk(m, body):
        p = piece_at(m)
        side = rem(side_of(m) + core, 2)

        def pair(s, carry):
            y2, x2, e, swap = place(p, partner(side, s))
            body(y2, x2, e)
            return carry

        lax.fori_loop(0, pair_count(m), pair, 0)

    def reduce_y(y2, x2, e):
        @pl.when(y2 == y)
        def _():
            total = own[x2, e]
            for r in range(1, ny):
                y3 = rem(y + r, ny)
                got = incoming.at[y3, x2, e]
                pltpu.make_async_copy(got, got, y_recv.at[y3, x2, e]).wait()
                total = total + incoming[y3, x2, e].astype(F32) * unscale[r]
            own[x2, e] = total
            for h in range(2):
                @pl.when((x2 != xlo) | (h != xhi))
                def _():
                    pltpu.make_async_remote_copy(
                        own.at[x2, e, pl.ds(h * (topics // 2), topics // 2)],
                        xin.at[xlo * 2 + xhi, e],
                        x_send,
                        x_recv.at[xlo * 2 + xhi, e],
                        device_id={"term": y * 4 + x2 * 2 + core, "topic": h * nz + z},
                        device_id_type=MESH,
                    ).start()

    def reduce_x(y2, x2, e):
        @pl.when((y2 == y) & (x2 == xlo))
        def _():
            total = own[xlo, e, pl.ds(xhi * (topics // 2), topics // 2), :]
            for r in range(1, 4):
                source = rem(xlo * 2 + xhi + r, 4)
                got = xin.at[source, e]
                pltpu.make_async_copy(got, got, x_recv.at[source, e]).wait()
                total = total + xin[source, e]
            xsum[e] = total
            send_z(e)

    def send_z(e):
        def send(s, carry):
            target = rem(z + s, nz)
            pltpu.make_async_remote_copy(
                xsum.at[e, pl.ds(target * slim, slim)], zin.at[z, e], z_send, z_recv,
                device_id={"topic": xhi * nz + target}, device_id_type=MESH,
            ).start()
            return carry

        lax.fori_loop(1, nz, send, 0)

    @pl.when(core == 1)
    def _():
        send_z(sets - 1)

    def steps(start, stop, first_lag, second_lag):
        def step(m, carry):
            if first_lag >= 0:
                arrive(m)
            if second_lag >= 1:
                walk(m - LAG_Y, reduce_y)
            if second_lag >= 2:
                walk(m - LAG_X, reduce_x)
            return carry

        lax.fori_loop(start, stop, step, 0)

    steps(0, LAG_Y, 0, 0)
    steps(LAG_Y, min(LAG_X, n), 0, 1)
    steps(LAG_X, n, 0, 2)
    share_codes(0, codes[...])
    steps(n, n + LAG_Y, -1, 2)

    def drain(m, carry):
        walk(m, reduce_x)
        return carry

    lax.fori_loop(n + LAG_Y - LAG_X, n, drain, 0)

    zin[z] = xsum[:, pl.ds(z * slim, slim), :]
    zparts = zin.at[pl.ds(0, nz - 1)]
    pltpu.make_async_copy(zparts, zparts, z_recv).wait()
    total = zin[0]
    for s in range(1, nz):
        total = total + zin[s]
    zsum[...] = total

    def send_slim(s, carry):
        target = piece_at(n - 1 - s)
        e1 = rem(target + n - quo(d, 2) - core, n)
        swap = quo(e1 + half - 1 + core, n)
        e = e1 + swap * (n - core - 2 * e1)

        @pl.when(target != t)
        def _():
            pltpu.make_async_remote_copy(
                zsum.at[e], tile.at[pl.ds(t * slim, slim)], t_send, t_recv,
                device_id={"topic": target}, device_id_type=MESH,
            ).start()

        return carry

    lax.fori_loop(0, n, send_slim, 0)
    role = rem(t + n - quo(d, 2) - core, n)
    swapped = quo(role + half - 1 + core, n)
    tile[pl.ds(t * slim, slim), :] = zsum[role + swapped * (n - core - 2 * role)]
    tparts = tile.at[pl.ds(0, topics - slim)]
    pltpu.make_async_copy(tparts, tparts, t_recv).wait()

    @pl.when(swapped == 0)
    def _():
        high, middle = split2(tile[...].T)
        gsend[:, :topics] = high
        gsend[:, topics:] = middle

    @pl.when(swapped != 0)
    def _():
        high, middle = split2(tile[...])
        gsend[:, :topics] = high
        gsend[:, topics:] = middle

    def spot(source):
        return pl.ds(rem(source + n - t, n) * topics, topics)

    def send_gram(s, carry):
        pltpu.make_async_remote_copy(
            gsend, gcol.at[spot(d)], g_send, g_recv.at[d],
            device_id={"term": rem(d + 2 * s, n)}, device_id_type=MESH,
        ).start()
        return carry

    lax.fori_loop(1, half, send_gram, 0)
    pltpu.make_async_remote_copy(
        gsend, gcol.at[spot(d)], g_send, g_recv.at[d],
        device_id={"term": sibling}, device_id_type=MESH,
    ).start()
    gcol[spot(d), :] = gsend[...]

    dparts = drecv.at[pl.ds(0, n - 1)]
    pltpu.make_async_copy(dparts, dparts, d_recv).wait()
    data = drecv[0]
    for s in range(1, n):
        data = data + drecv[s]

    def pass_gram(s, carry):
        source = rem(d + n - 2 * s, n)
        got = gcol.at[spot(source)]
        pltpu.make_async_copy(got, got, g_recv.at[source]).wait()
        pltpu.make_async_remote_copy(
            got, got, g_send, g_recv.at[source],
            device_id={"term": sibling}, device_id_type=MESH,
        ).start()
        return carry

    lax.fori_loop(1, half, pass_gram, 0)

    def take_gram(s, carry):
        source = rem(sibling + n - 2 * s, n)
        got = gcol.at[spot(source)]
        pltpu.make_async_copy(got, got, g_recv.at[source]).wait()
        return carry

    lax.fori_loop(0, half, take_gram, 0)

    current = codes[...]
    for step in range(ITERS):
        if step > 0:
            share_codes(step, current)
        cparts = cbuf.at[step, :, pl.ds(0, (n - 1) * topics)]
        pltpu.make_async_copy(cparts, cparts, c_recv.at[step]).wait()
        applied = dot(cbuf[step], gcol[...])
        applied = applied[:, :topics] + applied[:, topics:]
        applied = applied[:block] + applied[block:]
        current = current * data / (applied + EPSILON)

    fsend[...] = current

    def send_column(s, carry):
        target = piece_at(n - 1 - s)

        @pl.when((t != d) | (target != t))
        def _():
            pltpu.make_async_remote_copy(
                fsend, brow.at[d], fb_send, fb_recv,
                device_id={"term": t, "topic": target}, device_id_type=MESH,
            ).start()

        return carry

    lax.fori_loop(0, n, send_column, 0)
    def send_row(s, carry):
        pltpu.make_async_remote_copy(
            fsend, arow.at[d], fa_send, fa_recv,
            device_id={"term": rem(d + s, n)}, device_id_type=MESH,
        ).start()
        return carry

    lax.fori_loop(1, n, send_row, 0)

    codes_out[...] = current
    arow[d] = current
    choose = picks.T.astype(BF)

    sent = factor.at[pl.ds(0, rows - piece)]
    pltpu.make_async_copy(sent, sent, a2a_send).wait()
    pltpu.make_async_copy(factor, factor, core_send).wait()
    for c in range(2):
        @pl.when(core == c)
        def _():
            if ny > 1:
                y_part = outgoing.at[pl.ds(0, ny - 1), :, pl.ds(0, sets - c)]
                pltpu.make_async_copy(y_part, y_part, y_send).wait()
            x_part = xin.at[pl.ds(0, 3), pl.ds(0, sets - c)]
            pltpu.make_async_copy(x_part, x_part, x_send).wait()

    pltpu.make_async_copy(zparts, zparts, z_send).wait()
    pltpu.make_async_copy(tparts, tparts, t_send).wait()
    gparts = gcol.at[pl.ds(0, (n - 1) * topics)]
    pltpu.make_async_copy(gparts, gparts, g_send).wait()
    pltpu.make_async_copy(dparts, dparts, d_send).wait()
    for step in range(ITERS):
        cparts = cbuf.at[step, :, pl.ds(0, (n - 1) * topics)]
        pltpu.make_async_copy(cparts, cparts, c_send.at[step]).wait()

    aparts = arow.at[pl.ds(0, n - 1)]
    pltpu.make_async_copy(aparts, aparts, fa_recv).wait()
    whole = arow[...].reshape(n * block, topics)
    high, middle = split2(whole)
    share_of_one = 1.0 / (n * block)
    weights_out[:width, :] = (dot(choose, high) * share_of_one).astype(BF)
    weights_out[width:, :] = (dot(choose, middle) * share_of_one).astype(BF)
    a_high, a_middle = split2(whole.T)

    @pl.when(t == d)
    def _():
        brow[d] = current
        bparts = brow.at[pl.ds(0, n - 1)]
        pltpu.make_async_copy(bparts, bparts, fb_recv).wait()
        pltpu.make_async_copy(bparts, bparts, fb_send).wait()

    @pl.when(t != d)
    def _():
        pltpu.make_async_copy(brow, brow, fb_recv).wait()
        pltpu.make_async_copy(brow, brow, fb_send).wait()

    b_high, b_middle = split2(brow[...].reshape(n * block, topics))
    outer = dot(a_high, b_high) + (dot(a_high, b_middle) + dot(a_middle, b_high))
    gram_out[...] = DECAY * gram_stat[...] + outer * (1.0 / (n * block))
    pltpu.make_async_copy(aparts, aparts, fa_send).wait()


def statistic_kernel(
    parts, tiles, weights, stat, codes, gram, out, codes_out, gram_out,
    tiles_v, stat_v, out_v, tile_sem, stat_sem, out_sem,
):
    rows = tiles.shape[0] // parts

    def load(s):
        where = pl.ds(s * rows, rows)
        return (
            pltpu.make_async_copy(tiles.at[where], tiles_v.at[where], tile_sem.at[s]),
            pltpu.make_async_copy(stat.at[where], stat_v.at[where], stat_sem.at[s]),
        )

    def store(s):
        where = pl.ds(s * rows, rows)
        return pltpu.make_async_copy(out_v.at[where], out.at[where], out_sem.at[s])

    for s in range(parts):
        for copy in load(s):
            copy.start()
    codes_out[...] = codes[...]
    gram_out[...] = gram[...]
    for s in range(parts):
        for copy in load(s):
            copy.wait()
        where = pl.ds(s * rows, rows)
        part = tiles_v[where, :]
        out_v[where, :] = DECAY * stat_v[where, :] + dot(
            jnp.concatenate([part, part], axis=1), weights[...]
        )
        store(s).start()
    for s in range(parts):
        store(s).wait()


def per_device(n, factor, tile_values, tile_docs, codes, gram_stat, data_stat):
    rows, topics = factor.shape
    width = tile_values.shape[1]
    block = codes.shape[1]
    piece = rows // n
    sets = n // 2 + 1
    ny = n // 4
    nz = n // 2
    hbm = pl.BlockSpec(memory_space=pltpu.HBM)
    vmem = pl.BlockSpec(memory_space=pltpu.VMEM)
    dma = pltpu.SemaphoreType.DMA
    codes_t, gram, weights = pl.pallas_call(
        functools.partial(codes_kernel, n),
        out_shape=(
            jax.ShapeDtypeStruct((block, topics), F32),
            jax.ShapeDtypeStruct((topics, topics), F32),
            jax.ShapeDtypeStruct((2 * width, topics), BF),
        ),
        in_specs=[hbm] * 5,
        out_specs=(vmem, vmem, vmem),
        scratch_shapes=[
            pltpu.VMEM((rows, topics), BF),
            pltpu.VMEM((rows, width), BF),
            pltpu.VMEM((1, width), jnp.int32),
            pltpu.VMEM((block, topics), F32),
            pltpu.VMEM((topics, topics), F32),
            pltpu.VMEM((n, 2 * piece, topics), BF),
            pltpu.VMEM((2, n // 2, topics, 2 * piece), BF),
            pltpu.VMEM((n // 2, topics, topics), F32),
            pltpu.VMEM((2, sets, topics, topics), F32),
            pltpu.VMEM((ny, 2, sets, topics, topics), BF),
            pltpu.VMEM((ny, 2, sets, topics, topics), BF),
            pltpu.VMEM((4, sets, topics // 2, topics), F32),
            pltpu.VMEM((sets, topics // 2, topics), F32),
            pltpu.VMEM((nz, sets, topics // n, topics), F32),
            pltpu.VMEM((sets, topics // n, topics), F32),
            pltpu.VMEM((topics, topics), F32),
            pltpu.VMEM((n * topics, 2 * topics), BF),
            pltpu.VMEM((topics, 2 * topics), BF),
            pltpu.VMEM((ITERS, 2 * block, n * topics), BF),
            pltpu.VMEM((ITERS, 2 * block, topics), BF),
            pltpu.VMEM((n, block, topics), F32),
            pltpu.VMEM((n, block, topics), F32),
            pltpu.VMEM((block, topics), F32),
            pltpu.VMEM((n, block, topics), F32),
            pltpu.VMEM((n, block, topics), F32),
            dma((5,)), dma, dma((n,)), dma, dma((n,)), dma, dma((ny, 2, sets)),
            dma, dma((4, sets)), dma, dma, dma, dma, dma, dma((n,)), dma((ITERS,)), dma((ITERS,)),
            dma, dma, dma, dma, dma, dma,
        ],
        compiler_params=pltpu.CompilerParams(
            collective_id=0, has_side_effects=True, vmem_limit_bytes=62 * 1024 * 1024
        ),
        name="codes",
    )(factor, tile_values, tile_docs, codes.T, gram_stat)
    parts = PARTS
    data_new, codes_new, gram_new = pl.pallas_call(
        functools.partial(statistic_kernel, parts),
        out_shape=(
            jax.ShapeDtypeStruct((rows, topics), F32),
            jax.ShapeDtypeStruct((block, topics), F32),
            jax.ShapeDtypeStruct((topics, topics), F32),
        ),
        in_specs=[hbm, vmem, hbm, vmem, vmem],
        out_specs=(hbm, vmem, vmem),
        scratch_shapes=[
            pltpu.VMEM((rows, width), BF),
            pltpu.VMEM((rows, topics), F32),
            pltpu.VMEM((rows, topics), F32),
            dma((parts,)), dma((parts,)), dma((parts,)),
        ],
        compiler_params=pltpu.CompilerParams(vmem_limit_bytes=62 * 1024 * 1024),
        name="statistic",
    )(tile_values, weights, data_stat, codes_t, gram)
    return codes_new.T, gram_new, data_new


def solution(mesh):
    placed = (
        P("term", "topic"),
        P("term", None),
        P("term", None),
        P("topic", "term"),
        P("topic", "term"),
        P("term", "topic"),
    )
    return jax.shard_map(
        functools.partial(per_device, mesh.shape["term"]),
        mesh=mesh,
        in_specs=placed,
        out_specs=(P("topic", "term"), P("topic", "term"), P("term", "topic")),
        check_vma=False,
    )
```

```python
import functools

import jax
import jax.numpy as jnp
from jax import lax
from jax.experimental import pallas as pl
from jax.experimental.pallas import tpu as pltpu
from jax.sharding import PartitionSpec as P

ITERS = 3
EPSILON = 1e-06
DECAY = 0.5
PARTS = 4
LAG_Y = 3
LAG_X = 7
HOLD = 10
MESH = pl.DeviceIdType.MESH
BF = jnp.bfloat16
F32 = jnp.float32


def split2(value):
    high = value.astype(BF)
    return high, (value - high.astype(F32)).astype(BF)


def rem(value, count):
    return lax.rem(value, jnp.int32(count))


def quo(value, count):
    return lax.div(value, jnp.int32(count))


def dot(left, right):
    return jnp.dot(left, right, preferred_element_type=F32)


def codes_kernel(
    n, factor, tiles, docs_in, codes_in, gram_stat_in,
    codes_out, gram_out, weights_out,
    factor_v, tiles_v, docs, codes, gram_stat,
    xx, xt, product, own, outgoing, incoming, xin, xsum, zin, zsum, tile,
    gcol, gsend, cbuf, csend, dsend, drecv, fsend, arow, brow,
    local_sem, a2a_send, a2a_recv, core_send, core_recv, y_send, y_recv,
    x_send, x_recv, z_send, z_recv, t_send, t_recv, g_send, g_recv, c_send, c_recv,
    d_send, d_recv, fa_send, fa_recv, fb_send, fb_recv,
):
    rows, topics = factor.shape
    width = tiles.shape[1]
    piece = rows // n
    block = codes.shape[0]
    half = n // 2
    sets = half + 1
    group = min(4, half)
    ny = n // 4
    nz = n // 2
    slim = topics // n
    d = lax.axis_index("term")
    t = lax.axis_index("topic")
    core = rem(d, 2)
    xlo = rem(quo(d, 2), 2)
    y = quo(d, 4)
    xhi = quo(t, nz)
    z = rem(t, nz)
    sibling = d + 1 - 2 * core

    barrier = pltpu.get_barrier_semaphore()

    def greet(s, carry):
        pl.semaphore_signal(barrier, 1, device_id={"topic": rem(t + s, n)}, device_id_type=MESH)
        pl.semaphore_signal(barrier, 1, device_id={"term": rem(d + s, n)}, device_id_type=MESH)
        return carry

    lax.fori_loop(1, n, greet, 0)

    def greet_senders(s, carry):
        @pl.when((s != d) | (t != d))
        def _():
            pl.semaphore_signal(barrier, 1, device_id={"term": s, "topic": d}, device_id_type=MESH)
        return carry

    lax.fori_loop(0, n, greet_senders, 0)
    pl.semaphore_signal(
        barrier, 1,
        device_id={"term": y * 4 + (1 - xlo) * 2 + core, "topic": (1 - xhi) * nz + z},
        device_id_type=MESH,
    )
    loads = [
        pltpu.make_async_copy(a, b, local_sem.at[s])
        for s, (a, b) in enumerate(
            [(factor, factor_v), (tiles, tiles_v), (docs_in, docs), (codes_in, codes),
             (gram_stat_in, gram_stat)]
        )
    ]
    load_own = pltpu.make_async_copy(
        factor.at[pl.ds(t * piece, piece)], xx.at[t, pl.ds(core * piece, piece)], a2a_recv.at[t]
    )
    loads[3].start()
    load_own.start()
    for s in (0, 1, 2, 4):
        loads[s].start()

    @pl.when(t == d)
    def _():
        pl.semaphore_wait(barrier, 3 * n - 2)

    @pl.when(t != d)
    def _():
        pl.semaphore_wait(barrier, 3 * n - 1)

    def piece_at(m):
        u = quo(m, 2)
        odd = rem(u, 2)
        offset = odd * quo(u + 1, 2) + (1 - odd) * (nz - quo(u, 2))
        return rem(m, 2) * nz + rem(z + offset, nz)

    def send_piece(s, carry):
        p = piece_at(s)

        @pl.when(p != t)
        def _():
            pltpu.make_async_remote_copy(
                factor.at[pl.ds(p * piece, piece)],
                xx.at[t, pl.ds(core * piece, piece)],
                a2a_send,
                a2a_recv.at[t],
                device_id={"topic": p},
                device_id_type=MESH,
            ).start()

        return carry

    lax.fori_loop(0, n - 2, send_piece, 0)

    def share_codes(step, current):
        high, middle = split2(current)
        csend[step, :block, :] = high
        csend[step, block:, :] = middle

        def send_codes(s, carry):
            target = piece_at(n - 1 - s)

            @pl.when(target != t)
            def _():
                pltpu.make_async_remote_copy(
                    csend.at[step],
                    cbuf.at[step, :, pl.ds(pl.multiple_of(t * topics, topics), topics)],
                    c_send.at[step],
                    c_recv.at[step],
                    device_id={"topic": target},
                    device_id_type=MESH,
                ).start()

            return carry

        lax.fori_loop(0, n, send_codes, 0)
        cbuf[step, :, pl.ds(pl.multiple_of(t * topics, topics), topics)] = csend[step]


    for load in loads:
        load.wait()
    share = jnp.zeros((tiles.shape[1], topics), F32)
    for s in range(n):
        part = tiles_v[s * piece:(s + 1) * piece, :]
        share = share + lax.dot_general(
            part, factor_v[s * piece:(s + 1) * piece, :], (((0,), (0,)), ((), ())),
            preferred_element_type=F32,
        )
    picks = (
        lax.broadcasted_iota(jnp.int32, (n * block, tiles.shape[1]), 0) == docs[...]
    ).astype(F32)
    onehot = picks.astype(BF)
    high, middle = split2(share)
    low = (share - high.astype(F32) - middle.astype(F32)).astype(BF)
    spread = dot(onehot, high) + dot(onehot, middle) + dot(onehot, low)
    dsend[...] = spread.reshape(n, block, topics)

    def send_share(s, carry):
        target = rem(d + s, n)
        pltpu.make_async_remote_copy(
            dsend.at[target], drecv.at[d], d_send, d_recv,
            device_id={"term": target}, device_id_type=MESH,
        ).start()
        return carry

    lax.fori_loop(1, n, send_share, 0)
    drecv[d] = dsend[d]

    def place(p, q):
        k = rem(p + q, n)
        k_half = quo(k, 2)
        e1 = rem(p + n - k_half - core, n)
        swap = quo(e1 + half - 1 + core, n)
        e = e1 + swap * (n - core - 2 * e1)
        return quo(k_half, 2), rem(k_half, 2), e, swap

    def side_of(m):
        return rem(quo(quo(m, 2) + 1, 2), 2)

    def pair_count(m):
        u = quo(m, 2)
        return core * 2 * quo(u + 1, 2) + (1 - core) * (2 * quo(u, 2) + rem(m, 2) + 1)

    def partner(side, s):
        rank = quo(s, 2)
        return piece_at(4 * rank + 2 * rem(rank + side, 2) + rem(s, 2))

    def scale_of(y2):
        return 1.0 + ((y2 * 2 + xlo) * n + t).astype(F32) * (1.0 / (2 * ny * n))

    scale = scale_of(y)
    unscale = [1.0 / scale_of(rem(y + r, ny)) for r in range(ny)]
    xsum[sets - 1] = jnp.zeros((topics // 2, topics), F32)

    def arrive(m):
        p = piece_at(m)
        mine = xx.at[p, pl.ds(core * piece, piece)]
        theirs = xx.at[p, pl.ds((1 - core) * piece, piece)]
        pltpu.make_async_copy(mine, mine, a2a_recv.at[p]).wait()
        pltpu.make_async_remote_copy(
            mine, mine, core_send, core_recv.at[p],
            device_id={"term": sibling}, device_id_type=MESH,
        ).start()

        @pl.when(m == min(HOLD, n - 3))
        def _():
            lax.fori_loop(n - 2, n, send_piece, 0)

        pltpu.make_async_copy(theirs, theirs, core_recv.at[p]).wait()
        xt[side_of(m), 2 * quo(m, 4) + rem(m, 2)] = xx[p].T
        side = rem(side_of(m) + core, 2)
        count = pair_count(m)

        def multiply(g, carry):
            left = xt[side, pl.ds(g * group, group)].reshape(group * topics, 2 * piece)
            product[pl.ds(g * group, group)] = dot(left, xx[p]).reshape(group, topics, topics)
            return carry

        lax.fori_loop(0, quo(count + group - 1, group), multiply, 0)

        def pair(s, carry):
            y2, x2, e, swap = place(p, partner(side, s))

            @pl.when(swap == 0)
            def _():
                product[s] = product[s].T

            @pl.when(y2 == y)
            def _():
                own[x2, e] = product[s]

            @pl.when(y2 != y)
            def _():
                outgoing[y2, x2, e] = (product[s] * scale).astype(BF)
                pltpu.make_async_remote_copy(
                    outgoing.at[y2, x2, e], incoming.at[y, x2, e], y_send, y_recv.at[y, x2, e],
                    device_id={"term": y2 * 4 + xlo * 2 + core}, device_id_type=MESH,
                ).start()

            return carry

        lax.fori_loop(0, count, pair, 0)

    def walk(m, body):
        p = piece_at(m)
        side = rem(side_of(m) + core, 2)

        def pair(s, carry):
            y2, x2, e, swap = place(p, partner(side, s))
            body(y2, x2, e)
            return carry

        lax.fori_loop(0, pair_count(m), pair, 0)

    def reduce_y(y2, x2, e):
        @pl.when(y2 == y)
        def _():
            total = own[x2, e]
            for r in range(1, ny):
                y3 = rem(y + r, ny)
                got = incoming.at[y3, x2, e]
                pltpu.make_async_copy(got, got, y_recv.at[y3, x2, e]).wait()
                total = total + incoming[y3, x2, e].astype(F32) * unscale[r]
            own[x2, e] = total
            for h in range(2):
                @pl.when((x2 != xlo) | (h != xhi))
                def _():
                    pltpu.make_async_remote_copy(
                        own.at[x2, e, pl.ds(h * (topics // 2), topics // 2)],
                        xin.at[xlo * 2 + xhi, e],
                        x_send,
                        x_recv.at[xlo * 2 + xhi, e],
                        device_id={"term": y * 4 + x2 * 2 + core, "topic": h * nz + z},
                        device_id_type=MESH,
                    ).start()

    def reduce_x(y2, x2, e):
        @pl.when((y2 == y) & (x2 == xlo))
        def _():
            total = own[xlo, e, pl.ds(xhi * (topics // 2), topics // 2), :]
            for r in range(1, 4):
                source = rem(xlo * 2 + xhi + r, 4)
                got = xin.at[source, e]
                pltpu.make_async_copy(got, got, x_recv.at[source, e]).wait()
                total = total + xin[source, e]
            xsum[e] = total
            send_z(e)

    def send_z(e):
        def send(s, carry):
            target = rem(z + s, nz)
            pltpu.make_async_remote_copy(
                xsum.at[e, pl.ds(target * slim, slim)], zin.at[z, e], z_send, z_recv,
                device_id={"topic": xhi * nz + target}, device_id_type=MESH,
            ).start()
            return carry

        lax.fori_loop(1, nz, send, 0)

    @pl.when(core == 1)
    def _():
        send_z(sets - 1)

    def steps(start, stop, first_lag, second_lag):
        def step(m, carry):
            if first_lag >= 0:
                arrive(m)
            if second_lag >= 1:
                walk(m - LAG_Y, reduce_y)
            if second_lag >= 2:
                walk(m - LAG_X, reduce_x)
            return carry

        lax.fori_loop(start, stop, step, 0)

    steps(0, LAG_Y, 0, 0)
    steps(LAG_Y, min(LAG_X, n), 0, 1)
    steps(LAG_X, n, 0, 2)
    share_codes(0, codes[...])
    steps(n, n + LAG_Y, -1, 2)

    def drain(m, carry):
        walk(m, reduce_x)
        return carry

    lax.fori_loop(n + LAG_Y - LAG_X, n, drain, 0)

    zin[z] = xsum[:, pl.ds(z * slim, slim), :]
    zparts = zin.at[pl.ds(0, nz - 1)]
    pltpu.make_async_copy(zparts, zparts, z_recv).wait()
    total = zin[0]
    for s in range(1, nz):
        total = total + zin[s]
    zsum[...] = total

    def send_slim(s, carry):
        target = piece_at(n - 1 - s)
        e1 = rem(target + n - quo(d, 2) - core, n)
        swap = quo(e1 + half - 1 + core, n)
        e = e1 + swap * (n - core - 2 * e1)

        @pl.when(target != t)
        def _():
            pltpu.make_async_remote_copy(
                zsum.at[e], tile.at[pl.ds(t * slim, slim)], t_send, t_recv,
                device_id={"topic": target}, device_id_type=MESH,
            ).start()

        return carry

    lax.fori_loop(0, n, send_slim, 0)
    role = rem(t + n - quo(d, 2) - core, n)
    swapped = quo(role + half - 1 + core, n)
    tile[pl.ds(t * slim, slim), :] = zsum[role + swapped * (n - core - 2 * role)]
    tparts = tile.at[pl.ds(0, topics - slim)]
    pltpu.make_async_copy(tparts, tparts, t_recv).wait()

    @pl.when(swapped == 0)
    def _():
        high, middle = split2(tile[...].T)
        gsend[:, :topics] = high
        gsend[:, topics:] = middle

    @pl.when(swapped != 0)
    def _():
        high, middle = split2(tile[...])
        gsend[:, :topics] = high
        gsend[:, topics:] = middle

    def spot(source):
        return pl.ds(rem(source + n - t, n) * topics, topics)

    def send_gram(s, carry):
        pltpu.make_async_remote_copy(
            gsend, gcol.at[spot(d)], g_send, g_recv.at[d],
            device_id={"term": rem(d + 2 * s, n)}, device_id_type=MESH,
        ).start()
        return carry

    lax.fori_loop(1, half, send_gram, 0)
    pltpu.make_async_remote_copy(
        gsend, gcol.at[spot(d)], g_send, g_recv.at[d],
        device_id={"term": sibling}, device_id_type=MESH,
    ).start()
    gcol[spot(d), :] = gsend[...]

    dparts = drecv.at[pl.ds(0, n - 1)]
    pltpu.make_async_copy(dparts, dparts, d_recv).wait()
    data = drecv[0]
    for s in range(1, n):
        data = data + drecv[s]

    def pass_gram(s, carry):
        source = rem(d + n - 2 * s, n)
        got = gcol.at[spot(source)]
        pltpu.make_async_copy(got, got, g_recv.at[source]).wait()
        pltpu.make_async_remote_copy(
            got, got, g_send, g_recv.at[source],
            device_id={"term": sibling}, device_id_type=MESH,
        ).start()
        return carry

    lax.fori_loop(1, half, pass_gram, 0)

    def take_gram(s, carry):
        source = rem(sibling + n - 2 * s, n)
        got = gcol.at[spot(source)]
        pltpu.make_async_copy(got, got, g_recv.at[source]).wait()
        return carry

    lax.fori_loop(0, half, take_gram, 0)

    current = codes[...]
    for step in range(ITERS):
        if step > 0:
            share_codes(step, current)
        cparts = cbuf.at[step, :, pl.ds(0, (n - 1) * topics)]
        pltpu.make_async_copy(cparts, cparts, c_recv.at[step]).wait()
        applied = dot(cbuf[step], gcol[...])
        applied = applied[:, :topics] + applied[:, topics:]
        applied = applied[:block] + applied[block:]
        current = current * data / (applied + EPSILON)

    fsend[...] = current

    def send_column(s, carry):
        target = piece_at(n - 1 - s)

        @pl.when((t != d) | (target != t))
        def _():
            pltpu.make_async_remote_copy(
                fsend, brow.at[d], fb_send, fb_recv,
                device_id={"term": t, "topic": target}, device_id_type=MESH,
            ).start()

        return carry

    lax.fori_loop(0, n, send_column, 0)
    def send_row(s, carry):
        pltpu.make_async_remote_copy(
            fsend, arow.at[d], fa_send, fa_recv,
            device_id={"term": rem(d + s, n)}, device_id_type=MESH,
        ).start()
        return carry

    lax.fori_loop(1, n, send_row, 0)

    codes_out[...] = current
    arow[d] = current
    choose = picks.T.astype(BF)

    sent = factor.at[pl.ds(0, rows - piece)]
    pltpu.make_async_copy(sent, sent, a2a_send).wait()
    pltpu.make_async_copy(factor, factor, core_send).wait()
    for c in range(2):
        @pl.when(core == c)
        def _():
            if ny > 1:
                y_part = outgoing.at[pl.ds(0, ny - 1), :, pl.ds(0, sets - c)]
                pltpu.make_async_copy(y_part, y_part, y_send).wait()
            x_part = xin.at[pl.ds(0, 3), pl.ds(0, sets - c)]
            pltpu.make_async_copy(x_part, x_part, x_send).wait()

    pltpu.make_async_copy(zparts, zparts, z_send).wait()
    pltpu.make_async_copy(tparts, tparts, t_send).wait()
    gparts = gcol.at[pl.ds(0, (n - 1) * topics)]
    pltpu.make_async_copy(gparts, gparts, g_send).wait()
    pltpu.make_async_copy(dparts, dparts, d_send).wait()
    for step in range(ITERS):
        cparts = cbuf.at[step, :, pl.ds(0, (n - 1) * topics)]
        pltpu.make_async_copy(cparts, cparts, c_send.at[step]).wait()

    aparts = arow.at[pl.ds(0, n - 1)]
    pltpu.make_async_copy(aparts, aparts, fa_recv).wait()
    whole = arow[...].reshape(n * block, topics)
    high, middle = split2(whole)
    share_of_one = 1.0 / (n * block)
    weights_out[:width, :] = (dot(choose, high) * share_of_one).astype(BF)
    weights_out[width:, :] = (dot(choose, middle) * share_of_one).astype(BF)
    a_high, a_middle = split2(whole.T)

    @pl.when(t == d)
    def _():
        brow[d] = current
        bparts = brow.at[pl.ds(0, n - 1)]
        pltpu.make_async_copy(bparts, bparts, fb_recv).wait()
        pltpu.make_async_copy(bparts, bparts, fb_send).wait()

    @pl.when(t != d)
    def _():
        pltpu.make_async_copy(brow, brow, fb_recv).wait()
        pltpu.make_async_copy(brow, brow, fb_send).wait()

    b_high, b_middle = split2(brow[...].reshape(n * block, topics))
    outer = dot(a_high, b_high) + (dot(a_high, b_middle) + dot(a_middle, b_high))
    gram_out[...] = DECAY * gram_stat[...] + outer * (1.0 / (n * block))
    pltpu.make_async_copy(aparts, aparts, fa_send).wait()


def statistic_kernel(
    parts, tiles, weights, stat, codes, gram, out, codes_out, gram_out,
    tiles_v, stat_v, out_v, tile_sem, stat_sem, out_sem,
):
    rows = tiles.shape[0] // parts

    def load(s):
        where = pl.ds(s * rows, rows)
        return (
            pltpu.make_async_copy(tiles.at[where], tiles_v.at[where], tile_sem.at[s]),
            pltpu.make_async_copy(stat.at[where], stat_v.at[where], stat_sem.at[s]),
        )

    def store(s):
        where = pl.ds(s * rows, rows)
        return pltpu.make_async_copy(out_v.at[where], out.at[where], out_sem.at[s])

    for s in range(parts):
        for copy in load(s):
            copy.start()
    codes_out[...] = codes[...]
    gram_out[...] = gram[...]
    for s in range(parts):
        for copy in load(s):
            copy.wait()
        where = pl.ds(s * rows, rows)
        part = tiles_v[where, :]
        out_v[where, :] = DECAY * stat_v[where, :] + dot(
            jnp.concatenate([part, part], axis=1), weights[...]
        )
        store(s).start()
    for s in range(parts):
        store(s).wait()


def per_device(n, factor, tile_values, tile_docs, codes, gram_stat, data_stat):
    rows, topics = factor.shape
    width = tile_values.shape[1]
    block = codes.shape[1]
    piece = rows // n
    sets = n // 2 + 1
    ny = n // 4
    nz = n // 2
    hbm = pl.BlockSpec(memory_space=pltpu.HBM)
    vmem = pl.BlockSpec(memory_space=pltpu.VMEM)
    dma = pltpu.SemaphoreType.DMA
    codes_t, gram, weights = pl.pallas_call(
        functools.partial(codes_kernel, n),
        out_shape=(
            jax.ShapeDtypeStruct((block, topics), F32),
            jax.ShapeDtypeStruct((topics, topics), F32),
            jax.ShapeDtypeStruct((2 * width, topics), BF),
        ),
        in_specs=[hbm] * 5,
        out_specs=(vmem, vmem, vmem),
        scratch_shapes=[
            pltpu.VMEM((rows, topics), BF),
            pltpu.VMEM((rows, width), BF),
            pltpu.VMEM((1, width), jnp.int32),
            pltpu.VMEM((block, topics), F32),
            pltpu.VMEM((topics, topics), F32),
            pltpu.VMEM((n, 2 * piece, topics), BF),
            pltpu.VMEM((2, n // 2, topics, 2 * piece), BF),
            pltpu.VMEM((n // 2, topics, topics), F32),
            pltpu.VMEM((2, sets, topics, topics), F32),
            pltpu.VMEM((ny, 2, sets, topics, topics), BF),
            pltpu.VMEM((ny, 2, sets, topics, topics), BF),
            pltpu.VMEM((4, sets, topics // 2, topics), F32),
            pltpu.VMEM((sets, topics // 2, topics), F32),
            pltpu.VMEM((nz, sets, topics // n, topics), F32),
            pltpu.VMEM((sets, topics // n, topics), F32),
            pltpu.VMEM((topics, topics), F32),
            pltpu.VMEM((n * topics, 2 * topics), BF),
            pltpu.VMEM((topics, 2 * topics), BF),
            pltpu.VMEM((ITERS, 2 * block, n * topics), BF),
            pltpu.VMEM((ITERS, 2 * block, topics), BF),
            pltpu.VMEM((n, block, topics), F32),
            pltpu.VMEM((n, block, topics), F32),
            pltpu.VMEM((block, topics), F32),
            pltpu.VMEM((n, block, topics), F32),
            pltpu.VMEM((n, block, topics), F32),
            dma((5,)), dma, dma((n,)), dma, dma((n,)), dma, dma((ny, 2, sets)),
            dma, dma((4, sets)), dma, dma, dma, dma, dma, dma((n,)), dma((ITERS,)), dma((ITERS,)),
            dma, dma, dma, dma, dma, dma,
        ],
        compiler_params=pltpu.CompilerParams(
            collective_id=0, has_side_effects=True, vmem_limit_bytes=62 * 1024 * 1024
        ),
        name="codes",
    )(factor, tile_values, tile_docs, codes.T, gram_stat)
    parts = PARTS
    data_new, codes_new, gram_new = pl.pallas_call(
        functools.partial(statistic_kernel, parts),
        out_shape=(
            jax.ShapeDtypeStruct((rows, topics), F32),
            jax.ShapeDtypeStruct((block, topics), F32),
            jax.ShapeDtypeStruct((topics, topics), F32),
        ),
        in_specs=[hbm, vmem, hbm, vmem, vmem],
        out_specs=(hbm, vmem, vmem),
        scratch_shapes=[
            pltpu.VMEM((rows, width), BF),
            pltpu.VMEM((rows, topics), F32),
            pltpu.VMEM((rows, topics), F32),
            dma((parts,)), dma((parts,)), dma((parts,)),
        ],
        compiler_params=pltpu.CompilerParams(vmem_limit_bytes=62 * 1024 * 1024),
        name="statistic",
    )(tile_values, weights, data_stat, codes_t, gram)
    return codes_new.T, gram_new, data_new


def solution(mesh):
    placed = (
        P("term", "topic"),
        P("term", None),
        P("term", None),
        P("topic", "term"),
        P("topic", "term"),
        P("term", "topic"),
    )
    return jax.shard_map(
        functools.partial(per_device, mesh.shape["term"]),
        mesh=mesh,
        in_specs=placed,
        out_specs=(P("topic", "term"), P("topic", "term"), P("term", "topic")),
        check_vma=False,
    )
```

```python
import functools

import jax
import jax.numpy as jnp
from jax import lax
from jax.experimental import pallas as pl
from jax.experimental.pallas import tpu as pltpu
from jax.sharding import PartitionSpec as P

ITERS = 3
EPSILON = 1e-06
DECAY = 0.5
PARTS = 4
LAG_Y = 3
LAG_X = 7
HOLD = 10
MESH = pl.DeviceIdType.MESH
BF = jnp.bfloat16
F32 = jnp.float32


def split2(value):
    high = value.astype(BF)
    return high, (value - high.astype(F32)).astype(BF)


def rem(value, count):
    return lax.rem(value, jnp.int32(count))


def quo(value, count):
    return lax.div(value, jnp.int32(count))


def dot(left, right):
    return jnp.dot(left, right, preferred_element_type=F32)


def codes_kernel(
    n, factor, tiles, docs_in, codes_in, gram_stat_in,
    codes_out, gram_out, weights_out,
    factor_v, tiles_v, docs, codes, gram_stat,
    xx, xt, product, own, outgoing, incoming, xin, xsum, zin, zsum, tile,
    gcol, gsend, cbuf, csend, dsend, drecv, fsend, arow, brow,
    local_sem, a2a_send, a2a_recv, core_send, core_recv, y_send, y_recv,
    x_send, x_recv, z_send, z_recv, t_send, t_recv, g_send, g_recv, c_send, c_recv,
    d_send, d_recv, fa_send, fa_recv, fb_send, fb_recv,
):
    rows, topics = factor.shape
    width = tiles.shape[1]
    piece = rows // n
    block = codes.shape[0]
    half = n // 2
    sets = half + 1
    group = min(4, half)
    ny = n // 4
    nz = n // 2
    slim = topics // n
    d = lax.axis_index("term")
    t = lax.axis_index("topic")
    core = rem(d, 2)
    xlo = rem(quo(d, 2), 2)
    y = quo(d, 4)
    xhi = quo(t, nz)
    z = rem(t, nz)
    sibling = d + 1 - 2 * core

    barrier = pltpu.get_barrier_semaphore()

    def greet(s, carry):
        pl.semaphore_signal(barrier, 1, device_id={"topic": rem(t + s, n)}, device_id_type=MESH)
        pl.semaphore_signal(barrier, 1, device_id={"term": rem(d + s, n)}, device_id_type=MESH)
        return carry

    lax.fori_loop(1, n, greet, 0)

    def greet_senders(s, carry):
        @pl.when((s != d) | (t != d))
        def _():
            pl.semaphore_signal(barrier, 1, device_id={"term": s, "topic": d}, device_id_type=MESH)
        return carry

    lax.fori_loop(0, n, greet_senders, 0)
    pl.semaphore_signal(
        barrier, 1,
        device_id={"term": y * 4 + (1 - xlo) * 2 + core, "topic": (1 - xhi) * nz + z},
        device_id_type=MESH,
    )
    loads = [
        pltpu.make_async_copy(a, b, local_sem.at[s])
        for s, (a, b) in enumerate(
            [(factor, factor_v), (tiles, tiles_v), (docs_in, docs), (codes_in, codes),
             (gram_stat_in, gram_stat)]
        )
    ]
    load_own = pltpu.make_async_copy(
        factor.at[pl.ds(t * piece, piece)], xx.at[t, pl.ds(core * piece, piece)], a2a_recv.at[t]
    )
    loads[3].start()
    load_own.start()
    for s in (0, 1, 2, 4):
        loads[s].start()

    @pl.when(t == d)
    def _():
        pl.semaphore_wait(barrier, 3 * n - 2)

    @pl.when(t != d)
    def _():
        pl.semaphore_wait(barrier, 3 * n - 1)

    def piece_at(m):
        u = quo(m, 2)
        odd = rem(u, 2)
        offset = odd * quo(u + 1, 2) + (1 - odd) * (nz - quo(u, 2))
        return rem(m, 2) * nz + rem(z + offset, nz)

    def send_piece(s, carry):
        p = piece_at(s)

        @pl.when(p != t)
        def _():
            pltpu.make_async_remote_copy(
                factor.at[pl.ds(p * piece, piece)],
                xx.at[t, pl.ds(core * piece, piece)],
                a2a_send,
                a2a_recv.at[t],
                device_id={"topic": p},
                device_id_type=MESH,
            ).start()

        return carry

    lax.fori_loop(0, n - 2, send_piece, 0)

    def share_codes(step, current):
        high, middle = split2(current)
        csend[step, :block, :] = high
        csend[step, block:, :] = middle

        def send_codes(s, carry):
            target = piece_at(n - 1 - s)

            @pl.when(target != t)
            def _():
                pltpu.make_async_remote_copy(
                    csend.at[step],
                    cbuf.at[step, :, pl.ds(pl.multiple_of(t * topics, topics), topics)],
                    c_send.at[step],
                    c_recv.at[step],
                    device_id={"topic": target},
                    device_id_type=MESH,
                ).start()

            return carry

        lax.fori_loop(0, n, send_codes, 0)
        cbuf[step, :, pl.ds(pl.multiple_of(t * topics, topics), topics)] = csend[step]


    for load in loads:
        load.wait()
    share = jnp.zeros((tiles.shape[1], topics), F32)
    for s in range(n):
        part = tiles_v[s * piece:(s + 1) * piece, :]
        share = share + lax.dot_general(
            part, factor_v[s * piece:(s + 1) * piece, :], (((0,), (0,)), ((), ())),
            preferred_element_type=F32,
        )
    picks = (
        lax.broadcasted_iota(jnp.int32, (n * block, tiles.shape[1]), 0) == docs[...]
    ).astype(F32)
    onehot = picks.astype(BF)
    high, middle = split2(share)
    low = (share - high.astype(F32) - middle.astype(F32)).astype(BF)
    spread = dot(onehot, high) + dot(onehot, middle) + dot(onehot, low)
    dsend[...] = spread.reshape(n, block, topics)

    def send_share(s, carry):
        target = rem(d + s, n)
        pltpu.make_async_remote_copy(
            dsend.at[target], drecv.at[d], d_send, d_recv,
            device_id={"term": target}, device_id_type=MESH,
        ).start()
        return carry

    lax.fori_loop(1, n, send_share, 0)
    drecv[d] = dsend[d]

    def place(p, q):
        k = rem(p + q, n)
        k_half = quo(k, 2)
        e1 = rem(p + n - k_half - core, n)
        swap = quo(e1 + half - 1 + core, n)
        e = e1 + swap * (n - core - 2 * e1)
        return quo(k_half, 2), rem(k_half, 2), e, swap

    def side_of(m):
        return rem(quo(quo(m, 2) + 1, 2), 2)

    def pair_count(m):
        u = quo(m, 2)
        return core * 2 * quo(u + 1, 2) + (1 - core) * (2 * quo(u, 2) + rem(m, 2) + 1)

    def partner(side, s):
        rank = quo(s, 2)
        return piece_at(4 * rank + 2 * rem(rank + side, 2) + rem(s, 2))

    def scale_of(y2):
        return 1.0 + ((y2 * 2 + xlo) * n + t).astype(F32) * (1.0 / (2 * ny * n))

    scale = scale_of(y)
    unscale = [1.0 / scale_of(rem(y + r, ny)) for r in range(ny)]
    xsum[sets - 1] = jnp.zeros((topics // 2, topics), F32)

    def arrive(m):
        p = piece_at(m)
        mine = xx.at[p, pl.ds(core * piece, piece)]
        theirs = xx.at[p, pl.ds((1 - core) * piece, piece)]
        pltpu.make_async_copy(mine, mine, a2a_recv.at[p]).wait()
        pltpu.make_async_remote_copy(
            mine, mine, core_send, core_recv.at[p],
            device_id={"term": sibling}, device_id_type=MESH,
        ).start()

        @pl.when(m == min(HOLD, n - 3))
        def _():
            lax.fori_loop(n - 2, n, send_piece, 0)

        pltpu.make_async_copy(theirs, theirs, core_recv.at[p]).wait()
        xt[side_of(m), 2 * quo(m, 4) + rem(m, 2)] = xx[p].T
        side = rem(side_of(m) + core, 2)
        count = pair_count(m)

        def multiply(g, carry):
            left = xt[side, pl.ds(g * group, group)].reshape(group * topics, 2 * piece)
            product[pl.ds(g * group, group)] = dot(left, xx[p]).reshape(group, topics, topics)
            return carry

        lax.fori_loop(0, quo(count + group - 1, group), multiply, 0)

        def pair(s, carry):
            y2, x2, e, swap = place(p, partner(side, s))

            @pl.when(swap == 0)
            def _():
                product[s] = product[s].T

            @pl.when(y2 == y)
            def _():
                own[x2, e] = product[s]

            @pl.when(y2 != y)
            def _():
                outgoing[y2, x2, e] = (product[s] * scale).astype(BF)
                pltpu.make_async_remote_copy(
                    outgoing.at[y2, x2, e], incoming.at[y, x2, e], y_send, y_recv.at[y, x2, e],
                    device_id={"term": y2 * 4 + xlo * 2 + core}, device_id_type=MESH,
                ).start()

            return carry

        lax.fori_loop(0, count, pair, 0)

    def walk(m, body):
        p = piece_at(m)
        side = rem(side_of(m) + core, 2)

        def pair(s, carry):
            y2, x2, e, swap = place(p, partner(side, s))
            body(y2, x2, e)
            return carry

        lax.fori_loop(0, pair_count(m), pair, 0)

    def reduce_y(y2, x2, e):
        @pl.when(y2 == y)
        def _():
            total = own[x2, e]
            for r in range(1, ny):
                y3 = rem(y + r, ny)
                got = incoming.at[y3, x2, e]
                pltpu.make_async_copy(got, got, y_recv.at[y3, x2, e]).wait()
                total = total + incoming[y3, x2, e].astype(F32) * unscale[r]
            own[x2, e] = total
            for h in range(2):
                @pl.when((x2 != xlo) | (h != xhi))
                def _():
                    pltpu.make_async_remote_copy(
                        own.at[x2, e, pl.ds(h * (topics // 2), topics // 2)],
                        xin.at[xlo * 2 + xhi, e],
                        x_send,
                        x_recv.at[xlo * 2 + xhi, e],
                        device_id={"term": y * 4 + x2 * 2 + core, "topic": h * nz + z},
                        device_id_type=MESH,
                    ).start()

    def reduce_x(y2, x2, e):
        @pl.when((y2 == y) & (x2 == xlo))
        def _():
            total = own[xlo, e, pl.ds(xhi * (topics // 2), topics // 2), :]
            for r in range(1, 4):
                source = rem(xlo * 2 + xhi + r, 4)
                got = xin.at[source, e]
                pltpu.make_async_copy(got, got, x_recv.at[source, e]).wait()
                total = total + xin[source, e]
            xsum[e] = total
            send_z(e)

    def send_z(e):
        def send(s, carry):
            target = rem(z + s, nz)
            pltpu.make_async_remote_copy(
                xsum.at[e, pl.ds(target * slim, slim)], zin.at[z, e], z_send, z_recv,
                device_id={"topic": xhi * nz + target}, device_id_type=MESH,
            ).start()
            return carry

        lax.fori_loop(1, nz, send, 0)

    @pl.when(core == 1)
    def _():
        send_z(sets - 1)

    def steps(start, stop, first_lag, second_lag):
        def step(m, carry):
            if first_lag >= 0:
                arrive(m)
            if second_lag >= 1:
                walk(m - LAG_Y, reduce_y)
            if second_lag >= 2:
                walk(m - LAG_X, reduce_x)
            return carry

        lax.fori_loop(start, stop, step, 0)

    steps(0, LAG_Y, 0, 0)
    steps(LAG_Y, min(LAG_X, n), 0, 1)
    steps(LAG_X, n, 0, 2)
    share_codes(0, codes[...])
    steps(n, n + LAG_Y, -1, 2)

    def drain(m, carry):
        walk(m, reduce_x)
        return carry

    lax.fori_loop(n + LAG_Y - LAG_X, n, drain, 0)

    zin[z] = xsum[:, pl.ds(z * slim, slim), :]
    zparts = zin.at[pl.ds(0, nz - 1)]
    pltpu.make_async_copy(zparts, zparts, z_recv).wait()
    total = zin[0]
    for s in range(1, nz):
        total = total + zin[s]
    zsum[...] = total

    def send_slim(s, carry):
        target = piece_at(n - 1 - s)
        e1 = rem(target + n - quo(d, 2) - core, n)
        swap = quo(e1 + half - 1 + core, n)
        e = e1 + swap * (n - core - 2 * e1)

        @pl.when(target != t)
        def _():
            pltpu.make_async_remote_copy(
                zsum.at[e], tile.at[pl.ds(t * slim, slim)], t_send, t_recv,
                device_id={"topic": target}, device_id_type=MESH,
            ).start()

        return carry

    lax.fori_loop(0, n, send_slim, 0)
    role = rem(t + n - quo(d, 2) - core, n)
    swapped = quo(role + half - 1 + core, n)
    tile[pl.ds(t * slim, slim), :] = zsum[role + swapped * (n - core - 2 * role)]
    tparts = tile.at[pl.ds(0, topics - slim)]
    pltpu.make_async_copy(tparts, tparts, t_recv).wait()

    @pl.when(swapped == 0)
    def _():
        high, middle = split2(tile[...].T)
        gsend[:, :topics] = high
        gsend[:, topics:] = middle

    @pl.when(swapped != 0)
    def _():
        high, middle = split2(tile[...])
        gsend[:, :topics] = high
        gsend[:, topics:] = middle

    def spot(source):
        return pl.ds(rem(source + n - t, n) * topics, topics)

    def send_gram(s, carry):
        pltpu.make_async_remote_copy(
            gsend, gcol.at[spot(d)], g_send, g_recv.at[d],
            device_id={"term": rem(d + 2 * s, n)}, device_id_type=MESH,
        ).start()
        return carry

    lax.fori_loop(1, half, send_gram, 0)
    pltpu.make_async_remote_copy(
        gsend, gcol.at[spot(d)], g_send, g_recv.at[d],
        device_id={"term": sibling}, device_id_type=MESH,
    ).start()
    gcol[spot(d), :] = gsend[...]

    dparts = drecv.at[pl.ds(0, n - 1)]
    pltpu.make_async_copy(dparts, dparts, d_recv).wait()
    data = drecv[0]
    for s in range(1, n):
        data = data + drecv[s]

    def pass_gram(s, carry):
        source = rem(d + n - 2 * s, n)
        got = gcol.at[spot(source)]
        pltpu.make_async_copy(got, got, g_recv.at[source]).wait()
        pltpu.make_async_remote_copy(
            got, got, g_send, g_recv.at[source],
            device_id={"term": sibling}, device_id_type=MESH,
        ).start()
        return carry

    lax.fori_loop(1, half, pass_gram, 0)

    def take_gram(s, carry):
        source = rem(sibling + n - 2 * s, n)
        got = gcol.at[spot(source)]
        pltpu.make_async_copy(got, got, g_recv.at[source]).wait()
        return carry

    lax.fori_loop(0, half, take_gram, 0)

    current = codes[...]
    for step in range(ITERS):
        if step > 0:
            share_codes(step, current)
        cparts = cbuf.at[step, :, pl.ds(0, (n - 1) * topics)]
        pltpu.make_async_copy(cparts, cparts, c_recv.at[step]).wait()
        applied = dot(cbuf[step], gcol[...])
        applied = applied[:, :topics] + applied[:, topics:]
        applied = applied[:block] + applied[block:]
        current = current * data / (applied + EPSILON)

    fsend[...] = current

    def send_column(s, carry):
        target = piece_at(n - 1 - s)

        @pl.when((t != d) | (target != t))
        def _():
            pltpu.make_async_remote_copy(
                fsend, brow.at[d], fb_send, fb_recv,
                device_id={"term": t, "topic": target}, device_id_type=MESH,
            ).start()

        return carry

    lax.fori_loop(0, n, send_column, 0)
    def send_row(s, carry):
        pltpu.make_async_remote_copy(
            fsend, arow.at[d], fa_send, fa_recv,
            device_id={"term": rem(d + s, n)}, device_id_type=MESH,
        ).start()
        return carry

    lax.fori_loop(1, n, send_row, 0)

    codes_out[...] = current
    arow[d] = current
    choose = picks.T.astype(BF)

    sent = factor.at[pl.ds(0, rows - piece)]
    pltpu.make_async_copy(sent, sent, a2a_send).wait()
    pltpu.make_async_copy(factor, factor, core_send).wait()
    for c in range(2):
        @pl.when(core == c)
        def _():
            if ny > 1:
                y_part = outgoing.at[pl.ds(0, ny - 1), :, pl.ds(0, sets - c)]
                pltpu.make_async_copy(y_part, y_part, y_send).wait()
            x_part = xin.at[pl.ds(0, 3), pl.ds(0, sets - c)]
            pltpu.make_async_copy(x_part, x_part, x_send).wait()

    pltpu.make_async_copy(zparts, zparts, z_send).wait()
    pltpu.make_async_copy(tparts, tparts, t_send).wait()
    gparts = gcol.at[pl.ds(0, (n - 1) * topics)]
    pltpu.make_async_copy(gparts, gparts, g_send).wait()
    pltpu.make_async_copy(dparts, dparts, d_send).wait()
    for step in range(ITERS):
        cparts = cbuf.at[step, :, pl.ds(0, (n - 1) * topics)]
        pltpu.make_async_copy(cparts, cparts, c_send.at[step]).wait()

    aparts = arow.at[pl.ds(0, n - 1)]
    pltpu.make_async_copy(aparts, aparts, fa_recv).wait()
    whole = arow[...].reshape(n * block, topics)
    high, middle = split2(whole)
    share_of_one = 1.0 / (n * block)
    weights_out[:width, :] = (dot(choose, high) * share_of_one).astype(BF)
    weights_out[width:, :] = (dot(choose, middle) * share_of_one).astype(BF)
    a_high, a_middle = split2(whole.T)

    @pl.when(t == d)
    def _():
        brow[d] = current
        bparts = brow.at[pl.ds(0, n - 1)]
        pltpu.make_async_copy(bparts, bparts, fb_recv).wait()
        pltpu.make_async_copy(bparts, bparts, fb_send).wait()

    @pl.when(t != d)
    def _():
        pltpu.make_async_copy(brow, brow, fb_recv).wait()
        pltpu.make_async_copy(brow, brow, fb_send).wait()

    b_high, b_middle = split2(brow[...].reshape(n * block, topics))
    outer = dot(a_high, b_high) + (dot(a_high, b_middle) + dot(a_middle, b_high))
    gram_out[...] = DECAY * gram_stat[...] + outer * (1.0 / (n * block))
    pltpu.make_async_copy(aparts, aparts, fa_send).wait()


def statistic_kernel(
    parts, tiles, weights, stat, codes, gram, out, codes_out, gram_out,
    tiles_v, stat_v, out_v, weights_v, tile_sem, stat_sem, out_sem, small_sem,
):
    rows = tiles.shape[0] // parts

    def load(s):
        where = pl.ds(s * rows, rows)
        return (
            pltpu.make_async_copy(tiles.at[where], tiles_v.at[where], tile_sem.at[s]),
            pltpu.make_async_copy(stat.at[where], stat_v.at[where], stat_sem.at[s]),
        )

    def store(s):
        where = pl.ds(s * rows, rows)
        return pltpu.make_async_copy(out_v.at[where], out.at[where], out_sem.at[s])

    small = [
        pltpu.make_async_copy(a, b, small_sem.at[s])
        for s, (a, b) in enumerate([(weights, weights_v), (codes, codes_out), (gram, gram_out)])
    ]
    small[0].start()
    for s in range(parts):
        for copy in load(s):
            copy.start()
    small[1].start()
    small[2].start()
    small[0].wait()
    for s in range(parts):
        for copy in load(s):
            copy.wait()
        where = pl.ds(s * rows, rows)
        part = tiles_v[where, :]
        out_v[where, :] = DECAY * stat_v[where, :] + dot(
            jnp.concatenate([part, part], axis=1), weights_v[...]
        )
        store(s).start()
    for s in range(parts):
        store(s).wait()
    small[1].wait()
    small[2].wait()


def per_device(n, factor, tile_values, tile_docs, codes, gram_stat, data_stat):
    rows, topics = factor.shape
    width = tile_values.shape[1]
    block = codes.shape[1]
    piece = rows // n
    sets = n // 2 + 1
    ny = n // 4
    nz = n // 2
    hbm = pl.BlockSpec(memory_space=pltpu.HBM)
    vmem = pl.BlockSpec(memory_space=pltpu.VMEM)
    dma = pltpu.SemaphoreType.DMA
    codes_t, gram, weights = pl.pallas_call(
        functools.partial(codes_kernel, n),
        out_shape=(
            jax.ShapeDtypeStruct((block, topics), F32),
            jax.ShapeDtypeStruct((topics, topics), F32),
            jax.ShapeDtypeStruct((2 * width, topics), BF),
        ),
        in_specs=[hbm] * 5,
        out_specs=(vmem, vmem, vmem),
        scratch_shapes=[
            pltpu.VMEM((rows, topics), BF),
            pltpu.VMEM((rows, width), BF),
            pltpu.VMEM((1, width), jnp.int32),
            pltpu.VMEM((block, topics), F32),
            pltpu.VMEM((topics, topics), F32),
            pltpu.VMEM((n, 2 * piece, topics), BF),
            pltpu.VMEM((2, n // 2, topics, 2 * piece), BF),
            pltpu.VMEM((n // 2, topics, topics), F32),
            pltpu.VMEM((2, sets, topics, topics), F32),
            pltpu.VMEM((ny, 2, sets, topics, topics), BF),
            pltpu.VMEM((ny, 2, sets, topics, topics), BF),
            pltpu.VMEM((4, sets, topics // 2, topics), F32),
            pltpu.VMEM((sets, topics // 2, topics), F32),
            pltpu.VMEM((nz, sets, topics // n, topics), F32),
            pltpu.VMEM((sets, topics // n, topics), F32),
            pltpu.VMEM((topics, topics), F32),
            pltpu.VMEM((n * topics, 2 * topics), BF),
            pltpu.VMEM((topics, 2 * topics), BF),
            pltpu.VMEM((ITERS, 2 * block, n * topics), BF),
            pltpu.VMEM((ITERS, 2 * block, topics), BF),
            pltpu.VMEM((n, block, topics), F32),
            pltpu.VMEM((n, block, topics), F32),
            pltpu.VMEM((block, topics), F32),
            pltpu.VMEM((n, block, topics), F32),
            pltpu.VMEM((n, block, topics), F32),
            dma((5,)), dma, dma((n,)), dma, dma((n,)), dma, dma((ny, 2, sets)),
            dma, dma((4, sets)), dma, dma, dma, dma, dma, dma((n,)), dma((ITERS,)), dma((ITERS,)),
            dma, dma, dma, dma, dma, dma,
        ],
        compiler_params=pltpu.CompilerParams(
            collective_id=0, has_side_effects=True, vmem_limit_bytes=62 * 1024 * 1024
        ),
        name="codes",
    )(factor, tile_values, tile_docs, codes.T, gram_stat)
    parts = PARTS
    data_new, codes_new, gram_new = pl.pallas_call(
        functools.partial(statistic_kernel, parts),
        out_shape=(
            jax.ShapeDtypeStruct((rows, topics), F32),
            jax.ShapeDtypeStruct((block, topics), F32),
            jax.ShapeDtypeStruct((topics, topics), F32),
        ),
        in_specs=[hbm] * 5,
        out_specs=(hbm, hbm, hbm),
        scratch_shapes=[
            pltpu.VMEM((rows, width), BF),
            pltpu.VMEM((rows, topics), F32),
            pltpu.VMEM((rows, topics), F32),
            pltpu.VMEM((2 * width, topics), BF),
            dma((parts,)), dma((parts,)), dma((parts,)), dma((3,)),
        ],
        compiler_params=pltpu.CompilerParams(vmem_limit_bytes=62 * 1024 * 1024),
        name="statistic",
    )(tile_values, weights, data_stat, codes_t, gram)
    return codes_new.T, gram_new, data_new


def solution(mesh):
    placed = (
        P("term", "topic"),
        P("term", None),
        P("term", None),
        P("topic", "term"),
        P("topic", "term"),
        P("term", "topic"),
    )
    return jax.shard_map(
        functools.partial(per_device, mesh.shape["term"]),
        mesh=mesh,
        in_specs=placed,
        out_specs=(P("topic", "term"), P("topic", "term"), P("term", "topic")),
        check_vma=False,
    )
```
